256 devices in a mesh: dp: 64 (over z, y, core), outer: 4 (over x).
Axes of the slice: x: 4, y: 4, z: 8, core: 2. Of those that a mesh axis runs over, the one named last changes fastest.
Arguments:
- grad: bfloat16 [256, 524288], P(('dp', 'outer')), may hold values from -24 to 24
- momentum: float32 [256, 524288], P(('dp', 'outer')), may hold values from -6 to 6
- error: float32 [256, 524288], P(('dp', 'outer')), may hold values from -4 to 4
- variance: float32 [524288], replicated, may hold values from 0.1 to 4
- server_error: float32 [524288], P(('dp', 'outer')), may hold values from -4 to 4
Outputs:
- update: float32 [524288], replicated
- worker_error: float32 [256, 524288], P(('dp', 'outer'))
- server_residue: float32 [524288], P(('dp', 'outer'))
The draws below stay inside these ranges and needn't reach their ends.
All inputs are finite; a program needn't handle non-finite values.
Results may differ from the reference program's by a relative error of at most 0.014.
Values may be sent and summed in bfloat16 or wider, within the bound.
A program may use at most 64 MiB of HBM per device.

```python
import math
import jax
import jax.numpy as jnp
from jax import lax

WORKERS = 256
BUCKET = 524288


def raised(entries, stream_key, source, target, shards_of, factor):
    def block_of(axis_at):
        return (jnp.arange(entries.shape[axis_at]) // (entries.shape[axis_at] // shards_of)).reshape((-1,) + (1,) * (entries.ndim - 1 - axis_at))

    one_side = jax.random.permutation(stream_key, shards_of)[block_of(target)]
    other_side = (block_of(target) + shards_of // 2) % shards_of
    return jnp.where((block_of(source) == one_side) | (block_of(source) == other_side), factor * entries, entries)


def block_levels(own_key, dims, pieces, low, top_value):
    level = 1.0
    for dim, shards_of in pieces:
        draws = jax.random.uniform(jax.random.fold_in(jax.random.fold_in(own_key, 6), dim), (shards_of,), jnp.float32, low / len(pieces), top_value / len(pieces))
        level = level * jnp.repeat(jnp.exp(draws), dims[dim] // shards_of).reshape((-1,) + (1,) * (len(dims) - 1 - dim))
    return level


def scatter_about(rng, extent, deviation, most, pieces=(), held_as=jnp.bfloat16):
    values = deviation * jax.random.normal(rng, extent, jnp.float32)
    if pieces:
        values = values * block_levels(rng, extent, pieces, -0.22, 0.18)
    return jnp.clip(values, -most, most).astype(held_as)


def bell_draw_with(rng, shape, scale, bound, shards, heavy, dtype=jnp.bfloat16):
    result = scale * jax.random.normal(rng, shape, jnp.float32)
    if shards:
        result = result * block_levels(rng, shape, shards, -0.22, 0.18)
    return jnp.clip(raised(result, jax.random.fold_in(rng, 3), *heavy), -bound, bound).astype(dtype)


def setup_inputs(seed: int = 0) -> dict:
    keys = jax.random.split(jax.random.key(seed), 6)
    return {
        "grad": bell_draw_with(keys[0], (WORKERS, BUCKET), 1.0, 24.0, ((0, 256),), (0, 1, 256, 6.0)),
        "momentum": scatter_about(keys[1], (WORKERS, BUCKET), 1.0, 6.0, ((0, 256),), jnp.float32),
        "error": scatter_about(keys[2], (WORKERS, BUCKET), 0.5, 4.0, ((0, 256),), jnp.float32),
        "variance": jnp.clip(jnp.exp(jax.random.uniform(keys[3], (BUCKET,), jnp.float32, math.log(0.1), math.log(4.0))), 0.1, 4.0),
        "server_error": scatter_about(keys[4], (BUCKET,), 0.5, 4.0, ((0, 256),), jnp.float32),
    }


def compress(values):
    blocks = values.reshape(-1, 128)
    spread = jnp.sqrt(lax.optimization_barrier(jnp.mean(blocks * blocks, axis=1, keepdims=True)) + 1e-06)
    return (spread * jnp.tanh(blocks / spread)).reshape(values.shape)

def reference(grad, momentum, error, variance, server_error):

    def step(summed, item):
        grad_row, moment_row, error_row = item
        compensated = 0.9 * moment_row + 0.1 * grad_row.astype(jnp.float32) + error_row
        sent = compress(compensated).astype(jnp.bfloat16).astype(jnp.float32)
        return (summed + sent, compensated - sent)
    summed, worker_error = lax.scan(step, jnp.zeros(grad.shape[1], jnp.float32), (grad, momentum, error))
    average = summed / grad.shape[0]
    shifted = average + server_error
    server_sent = compress(shifted).astype(jnp.bfloat16).astype(jnp.float32)
    server_residue = shifted - server_sent
    update = server_sent / (jnp.sqrt(variance) + 1e-08)
    return (update, worker_error, server_residue)
```

```python
import functools

import jax
import jax.numpy as jnp
from jax import lax
from jax.experimental import pallas as pl
from jax.experimental.pallas import tpu as pltpu
from jax.sharding import PartitionSpec as P

MESH = pl.DeviceIdType.MESH
NX, NY, NZ = 4, 4, 8
SPAN = 16
CHUNK = 2 * NX * NY * SPAN
ROWS = NZ * CHUNK
AHEAD = 6
LAG1 = 2
LAG2 = 5
GLAG1 = 3
GLAG2 = 5


def compress(values):
    power = jnp.mean(values * values, axis=-1, keepdims=True) + 1e-6
    inverse = lax.rsqrt(power)
    return power * inverse * jnp.tanh(values * inverse)


def kernel(
    grad_hbm, momentum_hbm, error_hbm, variance_hbm, server_error_hbm,
    update, worker_error, server_residue,
    grad, momentum, error, scale, server_error, residue,
    sent, from_core, chip_sum, from_a1, a1_sum, from_z, partial_sum, gathered,
    in_sem, small_sem, server_send, server_recv,
    core_send, core_recv, a1_send, a1_recv, z_send, z_recv, a2_send, a2_recv,
    gz_send, gz_recv, ga_send, ga_recv, gc_send, gc_recv,
):
    dp = lax.axis_index("dp")
    x = lax.axis_index("outer")
    c = lax.rem(dp, 2)
    y = lax.rem(lax.div(dp, 2), NY)
    z = lax.div(dp, 2 * NY)
    a1 = x + c * (y - x)
    a2 = y + c * (x - y)

    def at(px, py, pz, pc):
        return ((pz * NY + py) * 2 + pc, px)

    def on_a1(d):
        return at(lax.rem(x + d * (1 - c), NX), lax.rem(y + d * c, NY), z, c)

    def on_a2(d):
        return at(lax.rem(x + d * c, NX), lax.rem(y + d * (1 - c), NY), z, c)

    def on_z(d):
        return at(x, y, lax.rem(z + d, NZ), c)

    sibling = at(x, y, z, 1 - c)

    def remote(src, dst, send, recv, device):
        return pltpu.make_async_remote_copy(
            src, dst, send, recv, device_id=device, device_id_type=MESH
        )

    def landed(like, sem):
        pltpu.make_async_copy(like, like, sem).wait()

    barrier = pltpu.get_barrier_semaphore()
    peers = [sibling]
    peers += [on_a1(d) for d in (1, 2, 3)]
    peers += [on_a2(d) for d in (1, 2, 3)]
    peers += [on_z(d) for d in range(1, NZ)]
    for peer in peers:
        pl.semaphore_signal(barrier, inc=1, device_id=peer, device_id_type=MESH)

    def order(k):
        odd = lax.rem(k, 2)
        return 4 + (1 - odd) * lax.div(k, 2) - odd * lax.div(k + 1, 2)

    def plane(k):
        return lax.rem(z + order(k), NZ)

    def loads(k):
        pz = plane(k)
        rows = pl.ds(pl.multiple_of(pz * CHUNK, CHUNK), CHUNK)
        flat = pl.ds(pl.multiple_of(pz * (CHUNK * 128), CHUNK * 128), CHUNK * 128)
        return [
            pltpu.make_async_copy(grad_hbm.at[:, flat], grad.at[:, flat], in_sem.at[0, k]),
            pltpu.make_async_copy(momentum_hbm.at[rows], momentum.at[rows], in_sem.at[1, k]),
            pltpu.make_async_copy(error_hbm.at[rows], error.at[rows], in_sem.at[2, k]),
        ]

    def start_loads(k, _):
        for copy in loads(k):
            copy.start()
        return 0

    lax.fori_loop(0, NZ, start_loads, 0)
    load_server = pltpu.make_async_copy(server_error_hbm, server_error.at[a2], small_sem.at[0])
    load_server.start()
    load_variance = pltpu.make_async_copy(variance_hbm, scale, small_sem.at[1])
    load_variance.start()

    def compress_chunk(k):
        for copy in loads(k):
            copy.wait()
        pz = plane(k)
        for py in range(NY):
            first = pl.multiple_of(pz * CHUNK + py * 128, 128)
            flat = pl.ds(pl.multiple_of(first * 128, 128 * 128), 128 * 128)
            rows = pl.ds(first, 128)
            slope = grad[:, flat].astype(jnp.float32).reshape(128, 128)
            compensated = 0.9 * momentum[rows, :] + 0.1 * slope + error[rows, :]
            rounded = compress(compensated).astype(jnp.bfloat16)
            worker_error[rows, :] = compensated - rounded.astype(jnp.float32)
            for px in range(NX):
                sent[0, pz, px, py] = rounded[px * SPAN : (px + 1) * SPAN]
                sent[1, pz, py, px] = rounded[(NX + px) * SPAN : (NX + px + 1) * SPAN]

    def send_core(k):
        pz = plane(k)
        remote(sent.at[1 - c, pz], from_core.at[pz], core_send, core_recv.at[k], sibling).start()

    def sum_chip(k):
        pz = plane(k)
        landed(from_core.at[pz], core_recv.at[k])
        total = sent[c, pz].astype(jnp.float32) + from_core[pz].astype(jnp.float32)
        chip_sum[pz] = total.astype(jnp.bfloat16)
        for d in (2, 1, 3):
            to = lax.rem(a1 + d, 4)
            remote(
                chip_sum.at[pz, to], from_a1.at[pz, d - 1], a1_send, a1_recv.at[k], on_a1(d)
            ).start()

    def sum_a1(k):
        pz = plane(k)
        landed(from_a1.at[pz], a1_recv.at[k])
        total = chip_sum[pz, a1].astype(jnp.float32)
        for d in range(3):
            total += from_a1[pz, d].astype(jnp.float32)
        a1_sum[pz] = total.astype(jnp.bfloat16)

        @pl.when(k < NZ - 1)
        def _():
            d = order(k)
            remote(a1_sum.at[pz], from_z.at[d - 1], z_send, z_recv.at[d - 1], on_z(d)).start()

    def compress_only(k, _):
        compress_chunk(k)
        return 0

    def send_only(k, _):
        send_core(k)
        return 0

    def step(t, _):
        @pl.when(t < NZ)
        def _():
            compress_chunk(t)
            send_core(t)

        @pl.when(jnp.logical_and(t >= LAG1, t < NZ + LAG1))
        def _():
            sum_chip(t - LAG1)

        @pl.when(t >= LAG2)
        def _():
            sum_a1(t - LAG2)

        return 0

    lax.fori_loop(0, AHEAD, compress_only, 0)
    pl.semaphore_wait(barrier, len(peers))
    lax.fori_loop(0, AHEAD, send_only, 0)
    load_server.wait()
    for d in (2, 1, 3):
        remote(
            server_error.at[a2], server_error.at[a2], server_send, server_recv.at[d - 1], on_a2(d)
        ).start()

    def early(t, _):
        sum_chip(t)
        return 0

    if AHEAD > LAG1:
        lax.fori_loop(0, AHEAD - LAG1, early, 0)
    early_a1 = max(AHEAD - LAG2, 0)
    for k in range(early_a1):
        sum_a1(jnp.int32(k))
    lax.fori_loop(AHEAD, NZ + LAG2, step, 0)

    total = a1_sum[z].astype(jnp.float32)
    for d in range(NZ - 1):
        landed(from_z.at[d], z_recv.at[d])
        total += from_z[d].astype(jnp.float32)
    partial_sum[a2] = total.astype(jnp.bfloat16)
    for d in (2, 1, 3):
        remote(
            partial_sum.at[a2], partial_sum.at[a2], a2_send, a2_recv.at[d - 1], on_a2(d)
        ).start()

    load_variance.wait()

    def invert(i, _):
        rows = pl.ds(pl.multiple_of(i * 128, 128), 128)
        scale[rows, :] = 1.0 / (jnp.sqrt(scale[rows, :]) + 1e-8)
        return 0

    lax.fori_loop(0, ROWS // 128, invert, 0)

    for d in (1, 2, 3):
        landed(server_error.at[0], server_recv.at[d - 1])
    for d in (1, 2, 3):
        landed(partial_sum.at[0], a2_recv.at[d - 1])
    summed = partial_sum[0].astype(jnp.float32)
    for j in range(1, 4):
        summed += partial_sum[j].astype(jnp.float32)
    shifted = summed * (1.0 / (2 * NX * NY * NZ)) + server_error[...]
    answer = compress(shifted).astype(jnp.bfloat16)
    gathered[c, z, a1] = answer
    residue[...] = shifted - answer.astype(jnp.float32)

    mine = gathered.at[c, z, a1]
    for d in (4, 3, 5, 2, 6, 1, 7):
        remote(mine, mine, gz_send, gz_recv.at[d - 1], on_z(d)).start()
    server_residue[...] = residue[a2]

    def source(k):
        odd = lax.rem(k, 2)
        away = odd * lax.div(k + 1, 2) - (1 - odd) * lax.div(k, 2)
        return lax.rem(z + away + NZ, NZ)

    def forward_a1(k):
        pz = source(k)

        @pl.when(k > 0)
        def _():
            landed(gathered.at[c, pz, a1], gz_recv.at[lax.rem(z - pz + NZ, NZ) - 1])

        block = gathered.at[c, pz, a1]
        for d in (2, 1, 3):
            remote(block, block, ga_send, ga_recv.at[k], on_a1(d)).start()

    def finish(pz, pc):
        for py in range(NY):
            for px in range(NX):
                i1 = px + pc * (py - px)
                i2 = py + pc * (px - py)
                first = pz * CHUNK + py * 128 + pc * 64 + px * SPAN
                rows = pl.ds(pl.multiple_of(first, SPAN), SPAN)
                update[rows, :] = gathered[pc, pz, i1, i2].astype(jnp.float32) * scale[rows, :]

    def forward_core(k):
        pz = source(k)
        landed(from_a1.at[pz], ga_recv.at[k])
        block = gathered.at[c, pz]
        remote(block, block, gc_send, gc_recv.at[k], sibling).start()
        finish(pz, c)

    def last(k):
        pz = source(k)
        landed(gathered.at[1 - c, pz], gc_recv.at[k])
        finish(pz, 1 - c)

    def gather(t, _):
        @pl.when(t < NZ)
        def _():
            forward_a1(t)

        @pl.when(jnp.logical_and(t >= GLAG1, t < NZ + GLAG1))
        def _():
            forward_core(t - GLAG1)

        @pl.when(t >= GLAG2)
        def _():
            last(t - GLAG2)

        return 0

    lax.fori_loop(0, NZ + GLAG2, gather, 0)

    landed(from_core, core_send)
    landed(from_a1, a1_send)
    landed(from_z, z_send)
    landed(partial_sum.at[pl.ds(0, 3)], a2_send)
    landed(server_error.at[pl.ds(0, 3)], server_send)
    landed(from_z, gz_send)
    landed(from_a1, ga_send)
    landed(from_core, gc_send)


def local(grad, momentum, error, variance, server_error):
    f32, bf16, dma = jnp.float32, jnp.bfloat16, pltpu.SemaphoreType.DMA
    whole = (ROWS, 128)
    update, worker_error, server_residue = pl.pallas_call(
        kernel,
        name="exchange",
        out_shape=(
            pltpu.VMEM(whole, f32),
            pltpu.VMEM(whole, f32),
            pltpu.VMEM((SPAN, 128), f32),
        ),
        in_specs=[pl.BlockSpec(memory_space=pltpu.HBM)] * 5,
        out_specs=[pl.BlockSpec(memory_space=pltpu.VMEM)] * 3,
        scratch_shapes=[
            pltpu.VMEM((1, ROWS * 128), bf16),
            pltpu.VMEM(whole, f32),
            pltpu.VMEM(whole, f32),
            pltpu.VMEM(whole, f32),
            pltpu.VMEM((4, SPAN, 128), f32),
            pltpu.VMEM((4, SPAN, 128), f32),
            pltpu.VMEM((2, NZ, 4, 4, SPAN, 128), bf16),
            pltpu.VMEM((NZ, 4, 4, SPAN, 128), bf16),
            pltpu.VMEM((NZ, 4, 4, SPAN, 128), bf16),
            pltpu.VMEM((NZ, 3, 4, SPAN, 128), bf16),
            pltpu.VMEM((NZ, 4, SPAN, 128), bf16),
            pltpu.VMEM((NZ - 1, 4, SPAN, 128), bf16),
            pltpu.VMEM((4, 4, SPAN, 128), bf16),
            pltpu.VMEM((2, NZ, 4, 4, SPAN, 128), bf16),
            dma((3, NZ)),
            dma((2,)),
            dma, dma((3,)),
            dma, dma((NZ,)),
            dma, dma((NZ,)),
            dma, dma((NZ - 1,)),
            dma, dma((3,)),
            dma, dma((NZ - 1,)),
            dma, dma((NZ,)),
            dma, dma((NZ,)),
        ],
        compiler_params=pltpu.CompilerParams(
            collective_id=0, has_side_effects=True, vmem_limit_bytes=32 << 20
        ),
    )(
        *(
            pltpu.with_memory_space_constraint(operand, pltpu.HBM)
            for operand in (
                grad,
                momentum.reshape(whole),
                error.reshape(whole),
                variance.reshape(whole),
                server_error.reshape(SPAN, 128),
            )
        )
    )
    return (
        update.reshape(ROWS * 128),
        worker_error.reshape(1, ROWS * 128),
        server_residue.reshape(SPAN * 128),
    )


def solution(mesh):
    placed = (
        P(("dp", "outer"), None),
        P(("dp", "outer"), None),
        P(("dp", "outer"), None),
        P(),
        P(("dp", "outer")),
    )
    return jax.shard_map(
        local,
        mesh=mesh,
        in_specs=placed,
        out_specs=(P(), P(("dp", "outer"), None), P(("dp", "outer"))),
        check_vma=False,
    )
```

```python
import jax
import jax.numpy as jnp
from jax import lax
from jax.experimental import pallas as pl
from jax.experimental.pallas import tpu as pltpu
from jax.sharding import PartitionSpec as P

MESH = pl.DeviceIdType.MESH
NX, NY, NZ = 4, 4, 8
PLANE = NX * NY
SPAN = 16
CHUNK = 2 * PLANE * SPAN
ROWS = NZ * CHUNK
AHEAD = 1
LAG = 4
GLAG = 2
PARTS = 4

AWAY = sorted(
    ((dx, dy) for dx in range(NX) for dy in range(NY) if dx or dy),
    key=lambda d: -min(d[0], NX - d[0]) - min(d[1], NY - d[1]),
)
ABOVE = sorted(range(1, NZ), key=lambda d: -min(d, NZ - d))


def compress(values):
    power = jnp.mean(values * values, axis=-1, keepdims=True) + 1e-6
    inverse = lax.rsqrt(power)
    return power * inverse * jnp.tanh(values * inverse)


def kernel(
    grad_hbm, momentum_hbm, error_hbm, variance_hbm, server_error_hbm,
    update, worker_error, server_residue,
    grad, momentum, error, scale, server_error,
    sent, from_core, chip_sum, from_plane, plane_sum, gathered,
    in_sem, small_sem, server_send, server_recv,
    core_send, core_recv, plane_send, plane_recv, z_send, z_recv,
    gather_send, gather_recv, last_send, last_recv,
):
    dp = lax.axis_index("dp")
    x = lax.axis_index("outer")
    c = lax.rem(dp, 2)
    y = lax.rem(lax.div(dp, 2), NY)
    z = lax.div(dp, 2 * NY)

    def at(px, py, pz, pc):
        return ((pz * NY + py) * 2 + pc, px)

    sibling = at(x, y, z, 1 - c)
    plane = [(lax.rem(x + dx, NX), lax.rem(y + dy, NY)) for dx, dy in AWAY]
    column = [at(x, y, lax.rem(z + d, NZ), c) for d in ABOVE]
    me = y * NX + x

    def remote(src, dst, send, recv, device):
        return pltpu.make_async_remote_copy(
            src, dst, send, recv, device_id=device, device_id_type=MESH
        )

    def landed(like, sem):
        pltpu.make_async_copy(like, like, sem).wait()

    def each(count, body):
        def step(k, _):
            body(k)
            return 0

        lax.fori_loop(0, count, step, 0)

    def loads(k):
        rows = pl.ds(pl.multiple_of(k * CHUNK, CHUNK), CHUNK)
        flat = pl.ds(pl.multiple_of(k * (CHUNK * 128), CHUNK * 128), CHUNK * 128)
        return [
            pltpu.make_async_copy(grad_hbm.at[:, flat], grad.at[:, flat], in_sem.at[0, k]),
            pltpu.make_async_copy(momentum_hbm.at[rows], momentum.at[rows], in_sem.at[1, k]),
            pltpu.make_async_copy(error_hbm.at[rows], error.at[rows], in_sem.at[2, k]),
        ]

    def start_loads(k):
        for copy in loads(k):
            copy.start()

    each(NZ, start_loads)
    load_server = pltpu.make_async_copy(server_error_hbm, server_error.at[z], small_sem.at[0])
    load_server.start()
    load_variance = pltpu.make_async_copy(variance_hbm, scale, small_sem.at[1])
    load_variance.start()

    barrier = pltpu.get_barrier_semaphore()
    peers = [sibling] + [at(px, py, z, c) for px, py in plane] + column
    for peer in peers:
        pl.semaphore_signal(barrier, inc=1, device_id=peer, device_id_type=MESH)

    def compress_chunk(k):
        for copy in loads(k):
            copy.wait()
        for py in range(NY):
            first = pl.multiple_of(k * CHUNK + py * 128, 128)
            flat = pl.ds(pl.multiple_of(first * 128, 128 * 128), 128 * 128)
            rows = pl.ds(first, 128)
            slope = grad[:, flat].astype(jnp.float32).reshape(128, 128)
            compensated = 0.9 * momentum[rows, :] + 0.1 * slope + error[rows, :]
            rounded = compress(compensated).astype(jnp.bfloat16)
            worker_error[rows, :] = compensated - rounded.astype(jnp.float32)
            for pc in range(2):
                for px in range(NX):
                    first = (pc * NX + px) * SPAN
                    sent[pc, k, py * NX + px] = rounded[first : first + SPAN]

    def send_core(k):
        remote(sent.at[1 - c, k], from_core.at[k], core_send, core_recv.at[k], sibling).start()

    def sum_chip(k):
        landed(from_core.at[k], core_recv.at[k])
        total = sent[c, k].astype(jnp.float32) + from_core[k].astype(jnp.float32)
        chip_sum[k] = total.astype(jnp.bfloat16)
        for px, py in plane:
            remote(
                chip_sum.at[k, py * NX + px],
                from_plane.at[k, me],
                plane_send,
                plane_recv.at[k],
                at(px, py, z, c),
            ).start()
        from_plane[k, me] = chip_sum[k, me]

    def sum_plane(k):
        landed(from_plane.at[k, pl.ds(0, PLANE - 1)], plane_recv.at[k])
        total = jnp.sum(from_plane[k].astype(jnp.float32), axis=0)
        plane_sum[k, z] = total.astype(jnp.bfloat16)
        block = plane_sum.at[k, z]
        for peer in column:
            remote(block, block, z_send, z_recv.at[k], peer).start()

    def serve(k):
        landed(plane_sum.at[k, pl.ds(0, NZ - 1)], z_recv.at[k])
        total = jnp.sum(plane_sum[k].astype(jnp.float32), axis=0)
        shifted = total * (1.0 / (2 * PLANE * NZ)) + server_error[k]
        answer = compress(shifted).astype(jnp.bfloat16)
        gathered[c, k, me] = answer
        block = gathered.at[c, k, me]
        for px, py in plane:
            remote(block, block, gather_send, gather_recv.at[k], at(px, py, z, c)).start()

        @pl.when(k == z)
        def _():
            server_residue[...] = shifted - answer.astype(jnp.float32)

    def finish(k, pc):
        for py in range(NY):
            first = pl.multiple_of(k * CHUNK + py * 128 + pc * 64, 64)
            rows = pl.ds(first, 64)
            values = gathered[pc, k, py * NX : (py + 1) * NX].astype(jnp.float32)
            update[rows, :] = values.reshape(64, 128) * scale[rows, :]

    def hand_over(k):
        landed(from_plane.at[k, pl.ds(0, PLANE - 1)], gather_recv.at[k])
        block = gathered.at[c, k]
        remote(block, block, last_send, last_recv.at[k], sibling).start()
        finish(k, c)

    def take_over(k):
        landed(gathered.at[1 - c, k], last_recv.at[k])
        finish(k, 1 - c)

    each(AHEAD, compress_chunk)
    pl.semaphore_wait(barrier, len(peers))
    each(AHEAD, send_core)

    def early(t, _):
        @pl.when(t < NZ)
        def _():
            compress_chunk(t)
            send_core(t)

        @pl.when(t >= LAG)
        def _():
            sum_chip(t - LAG)

        return 0

    lax.fori_loop(AHEAD, NZ + LAG, early, 0)

    load_server.wait()
    for peer in column:
        remote(server_error.at[z], server_error.at[z], server_send, server_recv, peer).start()

    load_variance.wait()

    def invert(i):
        rows = pl.ds(pl.multiple_of(i * 128, 128), 128)
        scale[rows, :] = 1.0 / (jnp.sqrt(scale[rows, :]) + 1e-8)

    each(ROWS // 128, invert)
    each(NZ, sum_plane)
    landed(server_error.at[pl.ds(0, NZ - 1)], server_recv)
    each(NZ, serve)

    def late(t, _):
        @pl.when(t < NZ)
        def _():
            hand_over(t)

        @pl.when(t >= GLAG)
        def _():
            take_over(t - GLAG)

        return 0

    lax.fori_loop(0, NZ + GLAG, late, 0)

    landed(from_core, core_send)
    landed(from_plane.at[:, pl.ds(0, PLANE - 1)], plane_send)
    landed(plane_sum.at[:, pl.ds(0, NZ - 1)], z_send)
    landed(server_error.at[pl.ds(0, NZ - 1)], server_send)
    landed(from_plane.at[:, pl.ds(0, PLANE - 1)], gather_send)
    landed(from_core, last_send)


def store(update, worker_error, server_residue, *refs):
    outs, sem = refs[:3], refs[3]
    copies = []
    for i, (src, dst) in enumerate(zip((update, worker_error, server_residue), outs)):
        parts = PARTS if src.shape[0] == ROWS else 1
        rows = src.shape[0] // parts
        for j in range(parts):
            piece = pl.ds(j * rows, rows)
            copies.append(pltpu.make_async_copy(src.at[piece], dst.at[piece], sem.at[i, j]))
    for copy in copies:
        copy.start()
    for copy in copies:
        copy.wait()


def local(grad, momentum, error, variance, server_error):
    f32, bf16, dma = jnp.float32, jnp.bfloat16, pltpu.SemaphoreType.DMA
    whole = (ROWS, 128)
    held = pl.pallas_call(
        kernel,
        name="exchange",
        out_shape=(
            pltpu.VMEM(whole, f32),
            pltpu.VMEM(whole, f32),
            pltpu.VMEM((SPAN, 128), f32),
        ),
        in_specs=[pl.BlockSpec(memory_space=pltpu.HBM)] * 5,
        out_specs=[pl.BlockSpec(memory_space=pltpu.VMEM)] * 3,
        scratch_shapes=[
            pltpu.VMEM((1, ROWS * 128), bf16),
            pltpu.VMEM(whole, f32),
            pltpu.VMEM(whole, f32),
            pltpu.VMEM(whole, f32),
            pltpu.VMEM((NZ, SPAN, 128), f32),
            pltpu.VMEM((2, NZ, PLANE, SPAN, 128), bf16),
            pltpu.VMEM((NZ, PLANE, SPAN, 128), bf16),
            pltpu.VMEM((NZ, PLANE, SPAN, 128), bf16),
            pltpu.VMEM((NZ, PLANE, SPAN, 128), bf16),
            pltpu.VMEM((NZ, NZ, SPAN, 128), bf16),
            pltpu.VMEM((2, NZ, PLANE, SPAN, 128), bf16),
            dma((3, NZ)),
            dma((2,)),
            dma, dma,
            dma, dma((NZ,)),
            dma, dma((NZ,)),
            dma, dma((NZ,)),
            dma, dma((NZ,)),
            dma, dma((NZ,)),
        ],
        compiler_params=pltpu.CompilerParams(
            collective_id=0, has_side_effects=True, vmem_limit_bytes=32 << 20
        ),
    )(
        *(
            pltpu.with_memory_space_constraint(operand, pltpu.HBM)
            for operand in (
                grad,
                momentum.reshape(whole),
                error.reshape(whole),
                variance.reshape(whole),
                server_error.reshape(SPAN, 128),
            )
        )
    )
    update, worker_error, server_residue = pl.pallas_call(
        store,
        name="store",
        out_shape=tuple(jax.ShapeDtypeStruct(v.shape, v.dtype) for v in held),
        in_specs=[pl.BlockSpec(memory_space=pltpu.VMEM)] * 3,
        out_specs=[pl.BlockSpec(memory_space=pl.ANY)] * 3,
        scratch_shapes=[dma((3, PARTS))],
        compiler_params=pltpu.CompilerParams(vmem_limit_bytes=1 << 20),
    )(*(pltpu.with_memory_space_constraint(v, pltpu.VMEM) for v in held))
    return (
        update.reshape(ROWS * 128),
        worker_error.reshape(1, ROWS * 128),
        server_residue.reshape(SPAN * 128),
    )


def solution(mesh):
    placed = (
        P(("dp", "outer"), None),
        P(("dp", "outer"), None),
        P(("dp", "outer"), None),
        P(),
        P(("dp", "outer")),
    )
    return jax.shard_map(
        local,
        mesh=mesh,
        in_specs=placed,
        out_specs=(P(), P(("dp", "outer"), None), P(("dp", "outer"))),
        check_vma=False,
    )
```

```python
import jax
import jax.numpy as jnp
from jax import lax
from jax.experimental import pallas as pl
from jax.experimental.pallas import tpu as pltpu
from jax.sharding import PartitionSpec as P

MESH = pl.DeviceIdType.MESH
NX, NY, NZ = 4, 4, 8
PLANE = NX * NY
SPAN = 16
CHUNK = 2 * PLANE * SPAN
ROWS = NZ * CHUNK
GREET, MEET = 2, 4
BEFORE, READY = 6, 2
SPREAD, SERVE, SCATTER, HAND, TAKE = 0, 7, 7, 14, 16
PARTS = 1

AWAY = sorted(
    ((dx, dy) for dx in range(NX) for dy in range(NY) if dx or dy),
    key=lambda d: -min(d[0], NX - d[0]) - min(d[1], NY - d[1]),
)
ABOVE = sorted(range(1, NZ), key=lambda d: -min(d, NZ - d))


def compress(values):
    power = jnp.mean(values * values, axis=-1, keepdims=True) + 1e-6
    inverse = lax.rsqrt(power)
    return power * inverse * jnp.tanh(values * inverse)


def kernel(
    grad_hbm, momentum_hbm, error_hbm, variance_hbm, server_error_hbm,
    update, worker_error, server_residue,
    grad, momentum, error, scale, server_error, residue,
    sent, from_core, chip_sum, from_plane, plane_sum, gathered,
    in_sem, small_sem, server_send, server_recv,
    core_send, core_recv, plane_send, plane_recv, z_send, z_recv,
    gather_send, last_send, word,
):
    dp = lax.axis_index("dp")
    x = lax.axis_index("outer")
    c = lax.rem(dp, 2)
    y = lax.rem(lax.div(dp, 2), NY)
    z = lax.div(dp, 2 * NY)

    me = y * NX + x

    def at(px, py, pz, pc):
        return ((pz * NY + py) * 2 + pc, px)

    sibling = at(x, y, z, 1 - c)
    plane = [(lax.rem(x + dx, NX), lax.rem(y + dy, NY)) for dx, dy in AWAY]
    column = [lax.rem(z + d, NZ) for d in ABOVE]

    gather_recv, last_recv = in_sem.at[0], in_sem.at[1]

    def remote(src, dst, send, recv, device):
        return pltpu.make_async_remote_copy(
            src, dst, send, recv, device_id=device, device_id_type=MESH
        )

    def landed(like, sem):
        pltpu.make_async_copy(like, like, sem).wait()

    def each(first, end, body):
        def step(k, _):
            body(k)
            return 0

        lax.fori_loop(first, end, step, 0)

    def load_grad(k):
        flat = pl.ds(pl.multiple_of(k * (CHUNK * 128), CHUNK * 128), CHUNK * 128)
        return pltpu.make_async_copy(grad_hbm.at[:, flat], grad.at[:, flat], in_sem.at[0, k])

    def start_loads(k):
        load_grad(k).start()
        rows = pl.ds(pl.multiple_of(k * CHUNK, CHUNK), CHUNK)
        for src, dst in ((momentum_hbm, momentum), (error_hbm, error)):
            pltpu.make_async_copy(src.at[rows], dst.at[rows], in_sem.at[1, k]).start()

    start_loads(0)
    barrier = pltpu.get_barrier_semaphore()
    others = [(px, py, z) for px, py in plane] + [(x, y, pz) for pz in column]

    def signal(semaphore, device):
        pl.semaphore_signal(semaphore, inc=1, device_id=device, device_id_type=MESH)

    @pl.when(c == 0)
    def _():
        signal(barrier, sibling)

    for other in others:
        signal(barrier, at(*other, 0))

    load_server = pltpu.make_async_copy(server_error_hbm, server_error.at[z], small_sem.at[0])
    load_server.start()
    each(1, NZ, start_loads)
    load_variance = pltpu.make_async_copy(variance_hbm, scale, small_sem.at[1])
    load_variance.start()

    def compress_chunk(k):
        load_grad(k).wait()
        landed(momentum.at[pl.ds(0, 2 * CHUNK)], in_sem.at[1, k])
        for py in range(NY):
            first = pl.multiple_of(k * CHUNK + py * 128, 128)
            flat = pl.ds(pl.multiple_of(first * 128, 128 * 128), 128 * 128)
            rows = pl.ds(first, 128)
            slope = grad[:, flat].astype(jnp.float32).reshape(128, 128)
            compensated = 0.9 * momentum[rows, :] + 0.1 * slope + error[rows, :]
            rounded = compress(compensated).astype(jnp.bfloat16)
            worker_error[rows, :] = compensated - rounded.astype(jnp.float32)
            for pc in range(2):
                for px in range(NX):
                    first = (pc * NX + px) * SPAN
                    sent[pc, k, py * NX + px] = rounded[first : first + SPAN]

    def send_core(k):
        remote(sent.at[1 - c, k], from_core.at[k], core_send, core_recv.at[k], sibling).start()

    def sum_chip(k):
        landed(from_core.at[k], core_recv.at[k])
        total = sent[c, k].astype(jnp.float32) + from_core[k].astype(jnp.float32)
        chip_sum[k] = total.astype(jnp.bfloat16)
        from_plane[k, me] = chip_sum[k, me]

    def send_plane(k):
        for px, py in plane:
            src, dst = chip_sum.at[k, py * NX + px], from_plane.at[k, me]
            remote(src, dst, plane_send, plane_recv.at[k], at(px, py, z, c)).start()

    def to_plane(k, pz):
        block = plane_sum.at[k, z]
        remote(block, block, z_send, z_recv.at[k], at(x, y, pz, c)).start()

    def sum_plane(k):
        landed(from_plane.at[k, pl.ds(0, PLANE - 1)], plane_recv.at[k])
        total = jnp.sum(from_plane[k].astype(jnp.float32), axis=0)
        plane_sum[k, z] = total.astype(jnp.bfloat16)

        @pl.when(z != 0)
        def _():
            to_plane(k, 0)

    def spread(k):
        for pz in column:

            @pl.when(pz != 0)
            def _():
                to_plane(k, pz)

    def to_chip(k, px, py):
        block = gathered.at[c, k, me]
        remote(block, block, gather_send, gather_recv.at[k], at(px, py, z, c)).start()

    def serve(k):
        landed(plane_sum.at[k, pl.ds(0, NZ - 1)], z_recv.at[k])
        total = jnp.sum(plane_sum[k].astype(jnp.float32), axis=0)
        shifted = total * (1.0 / (2 * PLANE * NZ)) + server_error[k]
        answer = compress(shifted).astype(jnp.bfloat16)
        gathered[c, k, me] = answer

        @pl.when(me != 0)
        def _():
            to_chip(k, 0, 0)

        residue[k] = shifted - answer.astype(jnp.float32)

    def scatter(k):
        for px, py in plane:

            @pl.when(py * NX + px != 0)
            def _():
                to_chip(k, px, py)

    def finish(k, pc):
        for py in range(NY):
            first = pl.multiple_of(k * CHUNK + py * 128 + pc * 64, 64)
            rows = pl.ds(first, 64)
            values = gathered[pc, k, py * NX : (py + 1) * NX].astype(jnp.float32)
            update[rows, :] = values.reshape(64, 128) * scale[rows, :]

    def hand_over(k):
        landed(from_plane.at[k, pl.ds(0, PLANE - 1)], gather_recv.at[k])
        block = gathered.at[c, k]
        remote(block, block, last_send, last_recv.at[k], sibling).start()
        finish(k, c)

    def take_over(k):
        landed(gathered.at[1 - c, k], last_recv.at[k])
        finish(k, 1 - c)

    def compress_and_send(k):
        compress_chunk(k)
        send_core(k)

    def sum_and_send(k):
        sum_chip(k)
        send_plane(k)

    each(0, GREET, compress_chunk)

    @pl.when(c == 1)
    def _():
        pl.semaphore_wait(barrier, 1)
        signal(word, sibling)

    each(GREET, MEET, compress_chunk)

    @pl.when(c == 0)
    def _():
        pl.semaphore_wait(word, 1)

    each(0, MEET, send_core)
    each(MEET, BEFORE, compress_and_send)
    each(0, READY, sum_chip)

    @pl.when(c == 0)
    def _():
        pl.semaphore_wait(barrier, 2 * len(others))
        signal(word, sibling)

    @pl.when(c == 1)
    def _():
        pl.semaphore_wait(word, 1)

    each(0, READY, send_plane)
    load_server.wait()
    for pz in column:
        block = server_error.at[z]
        remote(block, block, server_send, server_recv, at(x, y, pz, c)).start()
    each(BEFORE, NZ, compress_and_send)
    each(READY, NZ, sum_and_send)

    load_variance.wait()

    def invert(i):
        rows = pl.ds(pl.multiple_of(i * 128, 128), 128)
        scale[rows, :] = 1.0 / (jnp.sqrt(scale[rows, :]) + 1e-8)

    each(0, ROWS // 128, invert)

    def late(t, _):
        @pl.when(t == SERVE)
        def _():
            landed(server_error.at[pl.ds(0, NZ - 1)], server_recv)

        for lag, task in (
            (0, sum_plane),
            (SPREAD, spread),
            (SERVE, serve),
            (SCATTER, scatter),
            (HAND, hand_over),
            (TAKE, take_over),
        ):

            @pl.when(jnp.logical_and(t >= lag, t < lag + NZ))
            def _():
                task(t - lag)

        return 0

    lax.fori_loop(0, NZ + TAKE, late, 0)
    server_residue[...] = residue[z]

    landed(from_core, core_send)
    landed(from_plane.at[:, pl.ds(0, PLANE - 1)], plane_send)
    landed(plane_sum.at[:, pl.ds(0, NZ - 1)], z_send)
    landed(server_error.at[pl.ds(0, NZ - 1)], server_send)
    landed(from_plane.at[:, pl.ds(0, PLANE - 1)], gather_send)
    landed(from_core, last_send)


def store(update, worker_error, server_residue, *refs):
    outs, sem = refs[:3], refs[3]
    copies = []
    for i, (src, dst) in enumerate(zip((update, worker_error, server_residue), outs)):
        parts = PARTS if src.shape[0] == ROWS else 1
        rows = src.shape[0] // parts
        for j in range(parts):
            piece = pl.ds(j * rows, rows)
            copies.append(pltpu.make_async_copy(src.at[piece], dst.at[piece], sem.at[i, j]))
    for copy in copies:
        copy.start()
    for copy in copies:
        copy.wait()


def local(grad, momentum, error, variance, server_error):
    f32, bf16, dma = jnp.float32, jnp.bfloat16, pltpu.SemaphoreType.DMA
    whole = (ROWS, 128)
    held = pl.pallas_call(
        kernel,
        name="exchange",
        out_shape=(
            pltpu.VMEM(whole, f32),
            pltpu.VMEM(whole, f32),
            pltpu.VMEM((SPAN, 128), f32),
        ),
        in_specs=[pl.BlockSpec(memory_space=pltpu.HBM)] * 5,
        out_specs=[pl.BlockSpec(memory_space=pltpu.VMEM)] * 3,
        scratch_shapes=[
            pltpu.VMEM((1, ROWS * 128), bf16),
            pltpu.VMEM(whole, f32),
            pltpu.VMEM(whole, f32),
            pltpu.VMEM(whole, f32),
            pltpu.VMEM((NZ, SPAN, 128), f32),
            pltpu.VMEM((NZ, SPAN, 128), f32),
            pltpu.VMEM((2, NZ, PLANE, SPAN, 128), bf16),
            pltpu.VMEM((NZ, PLANE, SPAN, 128), bf16),
            pltpu.VMEM((NZ, PLANE, SPAN, 128), bf16),
            pltpu.VMEM((NZ, PLANE, SPAN, 128), bf16),
            pltpu.VMEM((NZ, NZ, SPAN, 128), bf16),
            pltpu.VMEM((2, NZ, PLANE, SPAN, 128), bf16),
            dma((2, NZ)),
            dma((2,)),
            dma, dma,
            dma, dma((NZ,)),
            dma, dma((NZ,)),
            dma, dma((NZ,)),
            dma, dma,
            pltpu.SemaphoreType.REGULAR,
        ],
        compiler_params=pltpu.CompilerParams(
            collective_id=0, has_side_effects=True, vmem_limit_bytes=32 << 20
        ),
    )(
        *(
            pltpu.with_memory_space_constraint(operand, pltpu.HBM)
            for operand in (
                grad,
                momentum.reshape(whole),
                error.reshape(whole),
                variance.reshape(whole),
                server_error.reshape(SPAN, 128),
            )
        )
    )
    update, worker_error, server_residue = pl.pallas_call(
        store,
        name="store",
        out_shape=tuple(jax.ShapeDtypeStruct(v.shape, v.dtype) for v in held),
        in_specs=[pl.BlockSpec(memory_space=pltpu.VMEM)] * 3,
        out_specs=[pl.BlockSpec(memory_space=pl.ANY)] * 3,
        scratch_shapes=[dma((3, PARTS))],
        compiler_params=pltpu.CompilerParams(vmem_limit_bytes=1 << 20),
    )(*(pltpu.with_memory_space_constraint(v, pltpu.VMEM) for v in held))
    return (
        update.reshape(ROWS * 128),
        worker_error.reshape(1, ROWS * 128),
        server_residue.reshape(SPAN * 128),
    )


def solution(mesh):
    placed = (
        P(("dp", "outer"), None),
        P(("dp", "outer"), None),
        P(("dp", "outer"), None),
        P(),
        P(("dp", "outer")),
    )
    return jax.shard_map(
        local,
        mesh=mesh,
        in_specs=placed,
        out_specs=(P(), P(("dp", "outer"), None), P(("dp", "outer"))),
        check_vma=False,
    )
```

```python
import jax
import jax.numpy as jnp
from jax import lax
from jax.experimental import pallas as pl
from jax.experimental.pallas import tpu as pltpu
from jax.sharding import PartitionSpec as P

MESH = pl.DeviceIdType.MESH
NX, NY, NZ = 4, 4, 8
PLANE = NX * NY
SPAN = 16
CHUNK = 2 * PLANE * SPAN
ROWS = NZ * CHUNK
GREET, MEET = 2, 4
BEFORE, READY = 6, 2
PAIR = 1
STEPS = NZ // PAIR
FIRST = 1
YIELD = 0
DIRECT = 7
PACE = 0
SPREAD, SERVE, SCATTER, HAND, TAKE = 0, 7, 7, 14, 16
PARTS = 1

AWAY = sorted(
    ((dx, dy) for dx in range(NX) for dy in range(NY) if dx or dy),
    key=lambda d: -min(d[0], NX - d[0]) - min(d[1], NY - d[1]),
)
ABOVE = sorted(range(1, NZ), key=lambda d: -min(d, NZ - d))


def compress(values):
    power = jnp.mean(values * values, axis=-1, keepdims=True) + 1e-6
    inverse = lax.rsqrt(power)
    return power * inverse * jnp.tanh(values * inverse)


def kernel(
    grad_hbm, momentum_hbm, error_hbm, variance_hbm, server_error_hbm,
    update, worker_error, server_residue,
    grad, momentum, error, scale, server_error, residue,
    sent, from_core, chip_sum, from_plane, plane_sum, gathered,
    in_sem, small_sem, server_send, server_recv,
    core_send, core_recv, plane_send, plane_recv, z_send, z_recv,
    gather_send, last_send, word,
):
    dp = lax.axis_index("dp")
    x = lax.axis_index("outer")
    c = lax.rem(dp, 2)
    y = lax.rem(lax.div(dp, 2), NY)
    z = lax.div(dp, 2 * NY)

    me = y * NX + x

    def at(px, py, pz, pc):
        return ((pz * NY + py) * 2 + pc, px)

    sibling = at(x, y, z, 1 - c)
    plane = [(lax.rem(x + dx, NX), lax.rem(y + dy, NY)) for dx, dy in AWAY]
    column = [lax.rem(z + d, NZ) for d in ABOVE]

    gather_recv, last_recv = in_sem.at[0], in_sem.at[1]

    def remote(src, dst, send, recv, device):
        return pltpu.make_async_remote_copy(
            src, dst, send, recv, device_id=device, device_id_type=MESH
        )

    def landed(like, sem):
        pltpu.make_async_copy(like, like, sem).wait()

    def each(first, end, body):
        def step(k, _):
            body(k)
            return 0

        lax.fori_loop(first, end, step, 0)

    def load_grad(k):
        flat = pl.ds(pl.multiple_of(k * (CHUNK * 128), CHUNK * 128), CHUNK * 128)
        return pltpu.make_async_copy(grad_hbm.at[:, flat], grad.at[:, flat], in_sem.at[0, k])

    def start_loads(k):
        load_grad(k).start()
        rows = pl.ds(pl.multiple_of(k * CHUNK, CHUNK), CHUNK)
        for src, dst in ((momentum_hbm, momentum), (error_hbm, error)):
            pltpu.make_async_copy(src.at[rows], dst.at[rows], in_sem.at[1, k]).start()

    barrier = pltpu.get_barrier_semaphore()
    others = [(x, y, column[0]), *((px, py, z) for px, py in plane), *((x, y, pz) for pz in column[1:])]

    def signal(semaphore, device):
        pl.semaphore_signal(semaphore, inc=1, device_id=device, device_id_type=MESH)

    for other in others:
        signal(barrier, at(*other, 0))

    @pl.when(c == 0)
    def _():
        signal(barrier, sibling)

    start_loads(0)
    load_server = pltpu.make_async_copy(server_error_hbm, server_error.at[z], small_sem.at[0])
    load_server.start()
    each(1, NZ, start_loads)
    load_variance = pltpu.make_async_copy(variance_hbm, scale, small_sem.at[1])
    load_variance.start()

    def compress_chunk(k):
        load_grad(k).wait()
        landed(momentum.at[pl.ds(0, 2 * CHUNK)], in_sem.at[1, k])
        for py in range(NY):
            first = pl.multiple_of(k * CHUNK + py * 128, 128)
            flat = pl.ds(pl.multiple_of(first * 128, 128 * 128), 128 * 128)
            rows = pl.ds(first, 128)
            slope = grad[:, flat].astype(jnp.float32).reshape(128, 128)
            compensated = 0.9 * momentum[rows, :] + 0.1 * slope + error[rows, :]
            rounded = compress(compensated).astype(jnp.bfloat16)
            worker_error[rows, :] = compensated - rounded.astype(jnp.float32)
            for pc in range(2):
                for px in range(NX):
                    first = (pc * NX + px) * SPAN
                    sent[pc, k, py * NX + px] = rounded[first : first + SPAN]

    def send_core(k):
        remote(sent.at[1 - c, k], from_core.at[k], core_send, core_recv.at[k], sibling).start()

    def sum_chip(k):
        landed(from_core.at[k], core_recv.at[k])
        total = sent[c, k].astype(jnp.float32) + from_core[k].astype(jnp.float32)
        chip_sum[lax.div(k, PAIR), :, lax.rem(k, PAIR)] = total.astype(jnp.bfloat16)

    def together(i):
        return pl.ds(i * PAIR, PAIR)

    def members(i):
        return [i * PAIR + j for j in range(PAIR)]

    def send_plane(i):
        for px, py in plane:
            src, dst = chip_sum.at[i, py * NX + px], from_plane.at[i, me]
            remote(src, dst, plane_send, plane_recv.at[i], at(px, py, z, c)).start()
        from_plane[i, me] = chip_sum[i, me]

    def to_plane(i, pz):
        block = plane_sum.at[i, z]
        remote(block, block, z_send, z_recv.at[i], at(x, y, pz, c)).start()

    def sum_plane(i):
        landed(from_plane.at[i, pl.ds(0, PLANE - 1)], plane_recv.at[i])
        total = jnp.sum(from_plane[i].astype(jnp.float32), axis=0)
        plane_sum[i, z] = total.astype(jnp.bfloat16)

        @pl.when(z != 0)
        def _():
            to_plane(i, 0)

    def spread(i):
        for pz in column:

            @pl.when(pz != 0)
            def _():
                to_plane(i, pz)

    def to_chip(i, px, py):
        block = gathered.at[c, i, me]
        remote(block, block, gather_send, gather_recv.at[i], at(px, py, z, c)).start()

        @pl.when(i >= DIRECT)
        def _():
            remote(block, block, gather_send, last_recv.at[i], at(px, py, z, 1 - c)).start()

    def serve(i):
        landed(plane_sum.at[i, pl.ds(0, NZ - 1)], z_recv.at[i])
        total = jnp.sum(plane_sum[i].astype(jnp.float32), axis=0)
        shifted = total * (1.0 / (2 * PLANE * NZ)) + server_error[together(i)]
        answer = compress(shifted).astype(jnp.bfloat16)
        gathered[c, i, me] = answer
        residue[together(i)] = shifted - answer.astype(jnp.float32)

        @pl.when(me != 0)
        def _():
            to_chip(i, 0, 0)

    def scatter(i):
        for px, py in plane:

            @pl.when(py * NX + px != 0)
            def _():
                to_chip(i, px, py)

        @pl.when(i >= DIRECT)
        def _():
            block = gathered.at[c, i, me]
            remote(block, block, gather_send, last_recv.at[i], sibling).start()

    def finish(i, j, pc):
        for py in range(NY):
            first = pl.multiple_of((i * PAIR + j) * CHUNK + py * 128 + pc * 64, 64)
            rows = pl.ds(first, 64)
            values = gathered[pc, i, py * NX : (py + 1) * NX, j].astype(jnp.float32)
            update[rows, :] = values.reshape(64, 128) * scale[rows, :]

    def hand_over(i):
        landed(from_plane.at[i, pl.ds(0, PLANE - 1)], gather_recv.at[i])

        @pl.when(i < DIRECT)
        def _():
            block = gathered.at[c, i]
            remote(block, block, last_send, last_recv.at[i], sibling).start()

        for j in range(PAIR):
            finish(i, j, c)

    def take_over(i):
        landed(gathered.at[1 - c, i], last_recv.at[i])
        for j in range(PAIR):
            finish(i, j, 1 - c)

    def compress_and_send(k):
        compress_chunk(k)
        send_core(k)

    def sum_and_send(i):
        for k in members(i):
            sum_chip(k)
        send_plane(i)

    each(0, GREET, compress_chunk)

    @pl.when(c == 1)
    def _():
        pl.semaphore_wait(barrier, 1)
        signal(word, sibling)

    each(GREET, MEET, compress_chunk)

    @pl.when(c == 0)
    def _():
        pl.semaphore_wait(word, 1)

    each(0, MEET, send_core)
    each(MEET, BEFORE, compress_and_send)
    each(0, READY, sum_chip)

    @pl.when(c == 0)
    def _():
        pl.semaphore_wait(barrier, 2 * len(others))
        signal(word, sibling)

    @pl.when(c == 1)
    def _():
        pl.semaphore_wait(word, 1)

    each(0, READY // PAIR, send_plane)
    load_server.wait()
    for pz in column:
        block = server_error.at[z]
        remote(block, block, server_send, server_recv, at(x, y, pz, c)).start()
    each(BEFORE, NZ, compress_and_send)
    load_variance.wait()

    def invert(i):
        rows = pl.ds(pl.multiple_of(i * 128, 128), 128)
        scale[rows, :] = 1.0 / (jnp.sqrt(scale[rows, :]) + 1e-8)

    @pl.when(c == 1)
    def _():
        each(0, ROWS // 128, invert)

    each(READY // PAIR, STEPS, sum_and_send)

    @pl.when(c == 0)
    def _():
        each(0, ROWS // 128, invert)


    def late(t, _):
        @pl.when(t == SERVE)
        def _():
            landed(server_error.at[pl.ds(0, NZ - 1)], server_recv)

        for lag, task in (
            (0, sum_plane),
            (SPREAD + YIELD * c, spread),
            (SERVE, serve),
            (SCATTER, scatter),
            (HAND, hand_over),
            (TAKE, take_over),
        ):

            @pl.when(jnp.logical_and(t >= lag, t < lag + STEPS))
            def _():
                task(t - lag)

        return 0

    lax.fori_loop(0, STEPS + TAKE, late, 0)
    server_residue[...] = residue[z]

    landed(from_core, core_send)
    landed(from_plane.at[:, pl.ds(0, PLANE - 1)], plane_send)
    landed(plane_sum.at[:, pl.ds(0, NZ - 1)], z_send)
    landed(server_error.at[pl.ds(0, NZ - 1)], server_send)
    landed(from_plane.at[:, pl.ds(0, PLANE - 1)], gather_send)
    landed(gathered.at[0, pl.ds(0, DIRECT)], last_send)
    if DIRECT < STEPS:
        landed(gathered.at[0, pl.ds(0, STEPS - DIRECT)], gather_send)


def store(update, worker_error, server_residue, *refs):
    outs, sem = refs[:3], refs[3]
    copies = []
    for i, (src, dst) in enumerate(zip((update, worker_error, server_residue), outs)):
        parts = PARTS if src.shape[0] == ROWS else 1
        rows = src.shape[0] // parts
        for j in range(parts):
            piece = pl.ds(j * rows, rows)
            copies.append(pltpu.make_async_copy(src.at[piece], dst.at[piece], sem.at[i, j]))
    for copy in copies:
        copy.start()
    for copy in copies:
        copy.wait()


def local(grad, momentum, error, variance, server_error):
    f32, bf16, dma = jnp.float32, jnp.bfloat16, pltpu.SemaphoreType.DMA
    whole = (ROWS, 128)
    held = pl.pallas_call(
        kernel,
        name="exchange",
        out_shape=(
            pltpu.VMEM(whole, f32),
            pltpu.VMEM(whole, f32),
            pltpu.VMEM((SPAN, 128), f32),
        ),
        in_specs=[pl.BlockSpec(memory_space=pltpu.HBM)] * 5,
        out_specs=[pl.BlockSpec(memory_space=pltpu.VMEM)] * 3,
        scratch_shapes=[
            pltpu.VMEM((1, ROWS * 128), bf16),
            pltpu.VMEM(whole, f32),
            pltpu.VMEM(whole, f32),
            pltpu.VMEM(whole, f32),
            pltpu.VMEM((NZ, SPAN, 128), f32),
            pltpu.VMEM((NZ, SPAN, 128), f32),
            pltpu.VMEM((2, NZ, PLANE, SPAN, 128), bf16),
            pltpu.VMEM((NZ, PLANE, SPAN, 128), bf16),
            pltpu.VMEM((STEPS, PLANE, PAIR, SPAN, 128), bf16),
            pltpu.VMEM((STEPS, PLANE, PAIR, SPAN, 128), bf16),
            pltpu.VMEM((STEPS, NZ, PAIR, SPAN, 128), bf16),
            pltpu.VMEM((2, STEPS, PLANE, PAIR, SPAN, 128), bf16),
            dma((2, NZ)),
            dma((2,)),
            dma, dma,
            dma, dma((NZ,)),
            dma, dma((STEPS,)),
            dma, dma((STEPS,)),
            dma, dma,
            pltpu.SemaphoreType.REGULAR,
        ],
        compiler_params=pltpu.CompilerParams(
            collective_id=0, has_side_effects=True, vmem_limit_bytes=32 << 20
        ),
    )(
        *(
            pltpu.with_memory_space_constraint(operand, pltpu.HBM)
            for operand in (
                grad,
                momentum.reshape(whole),
                error.reshape(whole),
                variance.reshape(whole),
                server_error.reshape(SPAN, 128),
            )
        )
    )
    update, worker_error, server_residue = pl.pallas_call(
        store,
        name="store",
        out_shape=tuple(jax.ShapeDtypeStruct(v.shape, v.dtype) for v in held),
        in_specs=[pl.BlockSpec(memory_space=pltpu.VMEM)] * 3,
        out_specs=[pl.BlockSpec(memory_space=pl.ANY)] * 3,
        scratch_shapes=[dma((3, PARTS))],
        compiler_params=pltpu.CompilerParams(vmem_limit_bytes=1 << 20),
    )(*(pltpu.with_memory_space_constraint(v, pltpu.VMEM) for v in held))
    return (
        update.reshape(ROWS * 128),
        worker_error.reshape(1, ROWS * 128),
        server_residue.reshape(SPAN * 128),
    )


def solution(mesh):
    placed = (
        P(("dp", "outer"), None),
        P(("dp", "outer"), None),
        P(("dp", "outer"), None),
        P(),
        P(("dp", "outer")),
    )
    return jax.shard_map(
        local,
        mesh=mesh,
        in_specs=placed,
        out_specs=(P(), P(("dp", "outer"), None), P(("dp", "outer"))),
        check_vma=False,
    )
```

```python
import jax
import jax.numpy as jnp
from jax import lax
from jax.experimental import pallas as pl
from jax.experimental.pallas import tpu as pltpu
from jax.sharding import PartitionSpec as P

MESH = pl.DeviceIdType.MESH
NX, NY, NZ = 4, 4, 8
PLANE = NX * NY
SPAN = 16
CHUNK = 2 * PLANE * SPAN
ROWS = NZ * CHUNK
GREET, MEET = 1, 2
BEFORE, READY = 5, 2
PAIR = 1
STEPS = NZ // PAIR
DIRECT = 7
SPREAD, SERVE, SCATTER, HAND, TAKE = 0, 7, 7, 14, 16
PARTS = 1

AWAY = sorted(
    ((dx, dy) for dx in range(NX) for dy in range(NY) if dx or dy),
    key=lambda d: -min(d[0], NX - d[0]) - min(d[1], NY - d[1]),
)
ABOVE = sorted(range(1, NZ), key=lambda d: -min(d, NZ - d))


def compress(values):
    power = jnp.mean(values * values, axis=-1, keepdims=True) + 1e-6
    inverse = lax.rsqrt(power)
    return power * inverse * jnp.tanh(values * inverse)


def kernel(
    grad_hbm, momentum_hbm, error_hbm, variance_hbm, server_error_hbm,
    update, worker_error, server_residue,
    grad, momentum, error, scale, server_error, residue,
    sent, from_core, chip_sum, from_plane, plane_sum, gathered,
    in_sem, small_sem, server_send, server_recv,
    core_send, core_recv, plane_send, plane_recv, z_send, z_recv,
    gather_send, last_send, word,
):
    dp = lax.axis_index("dp")
    x = lax.axis_index("outer")
    c = lax.rem(dp, 2)
    y = lax.rem(lax.div(dp, 2), NY)
    z = lax.div(dp, 2 * NY)

    me = y * NX + x

    def at(px, py, pz, pc):
        return ((pz * NY + py) * 2 + pc, px)

    sibling = at(x, y, z, 1 - c)
    plane = [(lax.rem(x + dx, NX), lax.rem(y + dy, NY)) for dx, dy in AWAY]
    column = [lax.rem(z + d, NZ) for d in ABOVE]

    gather_recv, last_recv = in_sem.at[0], in_sem.at[1]

    def remote(src, dst, send, recv, device):
        return pltpu.make_async_remote_copy(
            src, dst, send, recv, device_id=device, device_id_type=MESH
        )

    def landed(like, sem):
        pltpu.make_async_copy(like, like, sem).wait()

    def each(first, end, body):
        def step(k, _):
            body(k)
            return 0

        lax.fori_loop(first, end, step, 0)

    def load_grad(k):
        flat = pl.ds(pl.multiple_of(k * (CHUNK * 128), CHUNK * 128), CHUNK * 128)
        return pltpu.make_async_copy(grad_hbm.at[:, flat], grad.at[:, flat], in_sem.at[0, k])

    def start_loads(k):
        load_grad(k).start()
        rows = pl.ds(pl.multiple_of(k * CHUNK, CHUNK), CHUNK)
        for src, dst in ((momentum_hbm, momentum), (error_hbm, error)):
            pltpu.make_async_copy(src.at[rows], dst.at[rows], in_sem.at[1, k]).start()

    barrier = pltpu.get_barrier_semaphore()
    others = [(x, y, column[0]), *((px, py, z) for px, py in plane), *((x, y, pz) for pz in column[1:])]

    def signal(semaphore, device):
        pl.semaphore_signal(semaphore, inc=1, device_id=device, device_id_type=MESH)

    for other in others:
        signal(barrier, at(*other, 0))

    @pl.when(c == 0)
    def _():
        signal(barrier, sibling)

    start_loads(0)
    load_server = pltpu.make_async_copy(server_error_hbm, server_error.at[z], small_sem.at[0])
    load_server.start()
    each(1, NZ, start_loads)
    load_variance = pltpu.make_async_copy(variance_hbm, scale, small_sem.at[1])
    load_variance.start()

    def compress_chunk(k):
        load_grad(k).wait()
        landed(momentum.at[pl.ds(0, 2 * CHUNK)], in_sem.at[1, k])
        for py in range(NY):
            first = pl.multiple_of(k * CHUNK + py * 128, 128)
            flat = pl.ds(pl.multiple_of(first * 128, 128 * 128), 128 * 128)
            rows = pl.ds(first, 128)
            slope = grad[:, flat].astype(jnp.float32).reshape(128, 128)
            compensated = 0.9 * momentum[rows, :] + 0.1 * slope + error[rows, :]
            rounded = compress(compensated).astype(jnp.bfloat16)
            worker_error[rows, :] = compensated - rounded.astype(jnp.float32)
            for pc in range(2):
                for px in range(NX):
                    first = (pc * NX + px) * SPAN
                    sent[pc, k, py * NX + px] = rounded[first : first + SPAN]

    def send_core(k):
        remote(sent.at[1 - c, k], from_core.at[k], core_send, core_recv.at[k], sibling).start()

    def sum_chip(k):
        landed(from_core.at[k], core_recv.at[k])
        total = sent[c, k].astype(jnp.float32) + from_core[k].astype(jnp.float32)
        chip_sum[lax.div(k, PAIR), :, lax.rem(k, PAIR)] = total.astype(jnp.bfloat16)

    def together(i):
        return pl.ds(i * PAIR, PAIR)

    def members(i):
        return [i * PAIR + j for j in range(PAIR)]

    def send_plane(i):
        for px, py in plane:
            src, dst = chip_sum.at[i, py * NX + px], from_plane.at[i, me]
            remote(src, dst, plane_send, plane_recv.at[i], at(px, py, z, c)).start()
        from_plane[i, me] = chip_sum[i, me]

    def to_plane(i, pz):
        block = plane_sum.at[i, z]
        remote(block, block, z_send, z_recv.at[i], at(x, y, pz, c)).start()

    def sum_plane(i):
        landed(from_plane.at[i, pl.ds(0, PLANE - 1)], plane_recv.at[i])
        total = jnp.sum(from_plane[i].astype(jnp.float32), axis=0)
        plane_sum[i, z] = total.astype(jnp.bfloat16)

        @pl.when(z != 0)
        def _():
            to_plane(i, 0)

    def spread(i):
        for pz in column:

            @pl.when(pz != 0)
            def _():
                to_plane(i, pz)

    def to_chip(i, px, py):
        block = gathered.at[c, i, me]
        remote(block, block, gather_send, gather_recv.at[i], at(px, py, z, c)).start()

        @pl.when(i >= DIRECT)
        def _():
            remote(block, block, gather_send, last_recv.at[i], at(px, py, z, 1 - c)).start()

    def serve(i):
        landed(plane_sum.at[i, pl.ds(0, NZ - 1)], z_recv.at[i])
        total = jnp.sum(plane_sum[i].astype(jnp.float32), axis=0)
        shifted = total * (1.0 / (2 * PLANE * NZ)) + server_error[together(i)]
        answer = compress(shifted).astype(jnp.bfloat16)
        gathered[c, i, me] = answer
        residue[together(i)] = shifted - answer.astype(jnp.float32)

        @pl.when(me != 0)
        def _():
            to_chip(i, 0, 0)

    def scatter(i):
        for px, py in plane:

            @pl.when(py * NX + px != 0)
            def _():
                to_chip(i, px, py)

        @pl.when(i >= DIRECT)
        def _():
            block = gathered.at[c, i, me]
            remote(block, block, gather_send, last_recv.at[i], sibling).start()

    def finish(i, j, pc):
        for py in range(NY):
            first = pl.multiple_of((i * PAIR + j) * CHUNK + py * 128 + pc * 64, 64)
            rows = pl.ds(first, 64)
            values = gathered[pc, i, py * NX : (py + 1) * NX, j].astype(jnp.float32)
            update[rows, :] = values.reshape(64, 128) * scale[rows, :]

    def hand_over(i):
        landed(from_plane.at[i, pl.ds(0, PLANE - 1)], gather_recv.at[i])

        @pl.when(i < DIRECT)
        def _():
            block = gathered.at[c, i]
            remote(block, block, last_send, last_recv.at[i], sibling).start()

        for j in range(PAIR):
            finish(i, j, c)

    def take_over(i):
        landed(gathered.at[1 - c, i], last_recv.at[i])
        for j in range(PAIR):
            finish(i, j, 1 - c)

    def compress_and_send(k):
        compress_chunk(k)
        send_core(k)

    def sum_and_send(i):
        for k in members(i):
            sum_chip(k)
        send_plane(i)

    each(0, GREET, compress_chunk)

    @pl.when(c == 1)
    def _():
        pl.semaphore_wait(barrier, 1)
        signal(word, sibling)

    each(GREET, MEET, compress_chunk)

    @pl.when(c == 0)
    def _():
        pl.semaphore_wait(word, 1)

    each(0, MEET, send_core)
    each(MEET, BEFORE, compress_and_send)
    each(0, READY, sum_chip)

    @pl.when(c == 0)
    def _():
        pl.semaphore_wait(barrier, 2 * len(others))
        signal(word, sibling)

    @pl.when(c == 1)
    def _():
        pl.semaphore_wait(word, 1)

    each(0, READY // PAIR, send_plane)
    load_server.wait()
    for pz in column:
        block = server_error.at[z]
        remote(block, block, server_send, server_recv, at(x, y, pz, c)).start()
    each(BEFORE, NZ, compress_and_send)
    load_variance.wait()

    def invert(i):
        rows = pl.ds(pl.multiple_of(i * 128, 128), 128)
        scale[rows, :] = 1.0 / (jnp.sqrt(scale[rows, :]) + 1e-8)

    @pl.when(c == 1)
    def _():
        each(0, ROWS // 128, invert)

    each(READY // PAIR, STEPS, sum_and_send)

    @pl.when(c == 0)
    def _():
        each(0, ROWS // 128, invert)


    def late(t, _):
        @pl.when(t == SERVE)
        def _():
            landed(server_error.at[pl.ds(0, NZ - 1)], server_recv)

        for lag, task in (
            (0, sum_plane),
            (SPREAD, spread),
            (SERVE, serve),
            (SCATTER, scatter),
            (HAND, hand_over),
            (TAKE, take_over),
        ):

            @pl.when(jnp.logical_and(t >= lag, t < lag + STEPS))
            def _():
                task(t - lag)

        return 0

    lax.fori_loop(0, STEPS + TAKE, late, 0)
    server_residue[...] = residue[z]

    landed(from_core, core_send)
    landed(from_plane.at[:, pl.ds(0, PLANE - 1)], plane_send)
    landed(plane_sum.at[:, pl.ds(0, NZ - 1)], z_send)
    landed(server_error.at[pl.ds(0, NZ - 1)], server_send)
    landed(from_plane.at[:, pl.ds(0, PLANE - 1)], gather_send)
    landed(gathered.at[0, pl.ds(0, DIRECT)], last_send)
    if DIRECT < STEPS:
        landed(gathered.at[0, pl.ds(0, STEPS - DIRECT)], gather_send)


def store(update, worker_error, server_residue, *refs):
    outs, sem = refs[:3], refs[3]
    copies = []
    for i, (src, dst) in enumerate(zip((update, worker_error, server_residue), outs)):
        parts = PARTS if src.shape[0] == ROWS else 1
        rows = src.shape[0] // parts
        for j in range(parts):
            piece = pl.ds(j * rows, rows)
            copies.append(pltpu.make_async_copy(src.at[piece], dst.at[piece], sem.at[i, j]))
    for copy in copies:
        copy.start()
    for copy in copies:
        copy.wait()


def local(grad, momentum, error, variance, server_error):
    f32, bf16, dma = jnp.float32, jnp.bfloat16, pltpu.SemaphoreType.DMA
    whole = (ROWS, 128)
    held = pl.pallas_call(
        kernel,
        name="exchange",
        out_shape=(
            pltpu.VMEM(whole, f32),
            pltpu.VMEM(whole, f32),
            pltpu.VMEM((SPAN, 128), f32),
        ),
        in_specs=[pl.BlockSpec(memory_space=pltpu.HBM)] * 5,
        out_specs=[pl.BlockSpec(memory_space=pltpu.VMEM)] * 3,
        scratch_shapes=[
            pltpu.VMEM((1, ROWS * 128), bf16),
            pltpu.VMEM(whole, f32),
            pltpu.VMEM(whole, f32),
            pltpu.VMEM(whole, f32),
            pltpu.VMEM((NZ, SPAN, 128), f32),
            pltpu.VMEM((NZ, SPAN, 128), f32),
            pltpu.VMEM((2, NZ, PLANE, SPAN, 128), bf16),
            pltpu.VMEM((NZ, PLANE, SPAN, 128), bf16),
            pltpu.VMEM((STEPS, PLANE, PAIR, SPAN, 128), bf16),
            pltpu.VMEM((STEPS, PLANE, PAIR, SPAN, 128), bf16),
            pltpu.VMEM((STEPS, NZ, PAIR, SPAN, 128), bf16),
            pltpu.VMEM((2, STEPS, PLANE, PAIR, SPAN, 128), bf16),
            dma((2, NZ)),
            dma((2,)),
            dma, dma,
            dma, dma((NZ,)),
            dma, dma((STEPS,)),
            dma, dma((STEPS,)),
            dma, dma,
            pltpu.SemaphoreType.REGULAR,
        ],
        compiler_params=pltpu.CompilerParams(
            collective_id=0, has_side_effects=True, vmem_limit_bytes=32 << 20
        ),
    )(
        *(
            pltpu.with_memory_space_constraint(operand, pltpu.HBM)
            for operand in (
                grad,
                momentum.reshape(whole),
                error.reshape(whole),
                variance.reshape(whole),
                server_error.reshape(SPAN, 128),
            )
        )
    )
    update, worker_error, server_residue = pl.pallas_call(
        store,
        name="store",
        out_shape=tuple(jax.ShapeDtypeStruct(v.shape, v.dtype) for v in held),
        in_specs=[pl.BlockSpec(memory_space=pltpu.VMEM)] * 3,
        out_specs=[pl.BlockSpec(memory_space=pl.ANY)] * 3,
        scratch_shapes=[dma((3, PARTS))],
        compiler_params=pltpu.CompilerParams(vmem_limit_bytes=1 << 20),
    )(*(pltpu.with_memory_space_constraint(v, pltpu.VMEM) for v in held))
    return (
        update.reshape(ROWS * 128),
        worker_error.reshape(1, ROWS * 128),
        server_residue.reshape(SPAN * 128),
    )


def solution(mesh):
    placed = (
        P(("dp", "outer"), None),
        P(("dp", "outer"), None),
        P(("dp", "outer"), None),
        P(),
        P(("dp", "outer")),
    )
    return jax.shard_map(
        local,
        mesh=mesh,
        in_specs=placed,
        out_specs=(P(), P(("dp", "outer"), None), P(("dp", "outer"))),
        check_vma=False,
    )
```

```python
import jax
import jax.numpy as jnp
from jax import lax
from jax.experimental import pallas as pl
from jax.experimental.pallas import tpu as pltpu
from jax.sharding import PartitionSpec as P

MESH = pl.DeviceIdType.MESH
NX, NY, NZ = 4, 4, 8
PLANE = NX * NY
SPAN = 16
CHUNK = 2 * PLANE * SPAN
ROWS = NZ * CHUNK
GREET, MEET = 1, 2
BEFORE, READY = 6, 2
PAIR = 1
STEPS = NZ // PAIR
DIRECT = 7
SPREAD, SERVE, SCATTER, HAND, TAKE = 0, 7, 7, 14, 16
PARTS = 1

AWAY = sorted(
    ((dx, dy) for dx in range(NX) for dy in range(NY) if dx or dy),
    key=lambda d: -min(d[0], NX - d[0]) - min(d[1], NY - d[1]),
)
ABOVE = sorted(range(1, NZ), key=lambda d: -min(d, NZ - d))


def compress(values):
    power = jnp.mean(values * values, axis=-1, keepdims=True) + 1e-6
    inverse = lax.rsqrt(power)
    return power * inverse * jnp.tanh(values * inverse)


def kernel(
    grad_hbm, momentum_hbm, error_hbm, variance_hbm, server_error_hbm,
    update, worker_error, server_residue,
    grad, momentum, error, scale, server_error, residue,
    sent, from_core, chip_sum, from_plane, plane_sum, gathered,
    in_sem, small_sem, server_recv,
    out_sem, core_recv, plane_recv, z_recv, word,
):
    dp = lax.axis_index("dp")
    x = lax.axis_index("outer")
    c = lax.rem(dp, 2)
    y = lax.rem(lax.div(dp, 2), NY)
    z = lax.div(dp, 2 * NY)

    me = y * NX + x

    def at(px, py, pz, pc):
        return ((pz * NY + py) * 2 + pc, px)

    sibling = at(x, y, z, 1 - c)
    plane = [(lax.rem(x + dx, NX), lax.rem(y + dy, NY)) for dx, dy in AWAY]
    column = [lax.rem(z + d, NZ) for d in ABOVE]

    gather_recv, last_recv = in_sem.at[0], in_sem.at[1]

    def remote(src, dst, send, recv, device):
        return pltpu.make_async_remote_copy(
            src, dst, send, recv, device_id=device, device_id_type=MESH
        )

    def landed(like, sem):
        pltpu.make_async_copy(like, like, sem).wait()

    def each(first, end, body):
        def step(k, _):
            body(k)
            return 0

        lax.fori_loop(first, end, step, 0)

    def load_grad(k):
        flat = pl.ds(pl.multiple_of(k * (CHUNK * 128), CHUNK * 128), CHUNK * 128)
        return pltpu.make_async_copy(grad_hbm.at[:, flat], grad.at[:, flat], in_sem.at[0, k])

    def start_loads(k):
        load_grad(k).start()
        rows = pl.ds(pl.multiple_of(k * CHUNK, CHUNK), CHUNK)
        for src, dst in ((momentum_hbm, momentum), (error_hbm, error)):
            pltpu.make_async_copy(src.at[rows], dst.at[rows], in_sem.at[1, k]).start()

    barrier = pltpu.get_barrier_semaphore()
    others = [(x, y, column[0]), *((px, py, z) for px, py in plane), *((x, y, pz) for pz in column[1:])]

    def signal(semaphore, device):
        pl.semaphore_signal(semaphore, inc=1, device_id=device, device_id_type=MESH)

    for other in others:
        signal(barrier, at(*other, 0))

    @pl.when(c == 0)
    def _():
        signal(barrier, sibling)

    start_loads(0)
    load_server = pltpu.make_async_copy(server_error_hbm, server_error.at[z], small_sem.at[0])
    load_server.start()
    each(1, NZ, start_loads)
    load_variance = pltpu.make_async_copy(variance_hbm, scale, small_sem.at[1])
    load_variance.start()

    def compress_chunk(k):
        load_grad(k).wait()
        landed(momentum.at[pl.ds(0, 2 * CHUNK)], in_sem.at[1, k])
        for py in range(NY):
            first = pl.multiple_of(k * CHUNK + py * 128, 128)
            flat = pl.ds(pl.multiple_of(first * 128, 128 * 128), 128 * 128)
            rows = pl.ds(first, 128)
            slope = grad[:, flat].astype(jnp.float32).reshape(128, 128)
            compensated = 0.9 * momentum[rows, :] + 0.1 * slope + error[rows, :]
            rounded = compress(compensated).astype(jnp.bfloat16)
            worker_error[rows, :] = compensated - rounded.astype(jnp.float32)
            for pc in range(2):
                for px in range(NX):
                    first = (pc * NX + px) * SPAN
                    sent[pc, k, py * NX + px] = rounded[first : first + SPAN]

    def send_core(i):
        both = pl.ds(2 * i, 2)
        remote(sent.at[1 - c, both], from_core.at[both], out_sem, core_recv.at[i], sibling).start()

    def sum_chip(k):
        @pl.when(lax.rem(k, 2) == 0)
        def _():
            landed(from_core.at[pl.ds(0, 2)], core_recv.at[lax.div(k, 2)])

        total = sent[c, k].astype(jnp.float32) + from_core[k].astype(jnp.float32)
        chip_sum[lax.div(k, PAIR), :, lax.rem(k, PAIR)] = total.astype(jnp.bfloat16)

    def together(i):
        return pl.ds(i * PAIR, PAIR)

    def members(i):
        return [i * PAIR + j for j in range(PAIR)]

    def send_plane(i):
        for px, py in plane:
            src, dst = chip_sum.at[i, py * NX + px], from_plane.at[i, me]
            remote(src, dst, out_sem, plane_recv.at[i], at(px, py, z, c)).start()
        from_plane[i, me] = chip_sum[i, me]

    def to_plane(i, pz):
        block = plane_sum.at[i, z]
        remote(block, block, out_sem, z_recv.at[i], at(x, y, pz, c)).start()

    def sum_plane(i):
        landed(from_plane.at[i, pl.ds(0, PLANE - 1)], plane_recv.at[i])
        total = jnp.sum(from_plane[i].astype(jnp.float32), axis=0)
        plane_sum[i, z] = total.astype(jnp.bfloat16)

        @pl.when(z != 0)
        def _():
            to_plane(i, 0)

    def spread(i):
        for pz in column:

            @pl.when(pz != 0)
            def _():
                to_plane(i, pz)

    def to_chip(i, px, py):
        block = gathered.at[c, i, me]
        remote(block, block, out_sem, gather_recv.at[i], at(px, py, z, c)).start()

        @pl.when(i >= DIRECT)
        def _():
            remote(block, block, out_sem, last_recv.at[i], at(px, py, z, 1 - c)).start()

    def serve(i):
        landed(plane_sum.at[i, pl.ds(0, NZ - 1)], z_recv.at[i])
        total = jnp.sum(plane_sum[i].astype(jnp.float32), axis=0)
        shifted = total * (1.0 / (2 * PLANE * NZ)) + server_error[together(i)]
        answer = compress(shifted).astype(jnp.bfloat16)
        gathered[c, i, me] = answer
        residue[together(i)] = shifted - answer.astype(jnp.float32)

        @pl.when(me != 0)
        def _():
            to_chip(i, 0, 0)

    def scatter(i):
        for px, py in plane:

            @pl.when(py * NX + px != 0)
            def _():
                to_chip(i, px, py)

        @pl.when(i >= DIRECT)
        def _():
            block = gathered.at[c, i, me]
            remote(block, block, out_sem, last_recv.at[i], sibling).start()

    def finish(i, j, pc):
        for py in range(NY):
            first = pl.multiple_of((i * PAIR + j) * CHUNK + py * 128 + pc * 64, 64)
            rows = pl.ds(first, 64)
            values = gathered[pc, i, py * NX : (py + 1) * NX, j].astype(jnp.float32)
            update[rows, :] = values.reshape(64, 128) * scale[rows, :]

    def hand_over(i):
        landed(from_plane.at[i, pl.ds(0, PLANE - 1)], gather_recv.at[i])

        @pl.when(i < DIRECT)
        def _():
            block = gathered.at[c, i]
            remote(block, block, out_sem, last_recv.at[i], sibling).start()

        for j in range(PAIR):
            finish(i, j, c)

    def take_over(i):
        landed(gathered.at[1 - c, i], last_recv.at[i])
        for j in range(PAIR):
            finish(i, j, 1 - c)

    def compress_and_send(k):
        compress_chunk(k)

        @pl.when(lax.rem(k, 2) == 1)
        def _():
            send_core(lax.div(k, 2))

    def sum_and_send(i):
        for k in members(i):
            sum_chip(k)
        send_plane(i)

    each(0, GREET, compress_chunk)

    @pl.when(c == 1)
    def _():
        pl.semaphore_wait(barrier, 1)
        signal(word, sibling)

    each(GREET, MEET, compress_chunk)

    @pl.when(c == 0)
    def _():
        pl.semaphore_wait(word, 1)

    each(0, MEET // 2, send_core)
    each(MEET, BEFORE, compress_and_send)
    each(0, READY, sum_chip)

    @pl.when(c == 0)
    def _():
        pl.semaphore_wait(barrier, 2 * len(others))
        signal(word, sibling)

    @pl.when(c == 1)
    def _():
        pl.semaphore_wait(word, 1)

    each(0, READY // PAIR, send_plane)
    load_server.wait()
    for pz in column:
        block = server_error.at[z]
        remote(block, block, out_sem, server_recv, at(x, y, pz, c)).start()
    each(BEFORE, NZ, compress_and_send)
    load_variance.wait()

    def invert(i):
        rows = pl.ds(pl.multiple_of(i * 128, 128), 128)
        scale[rows, :] = 1.0 / (jnp.sqrt(scale[rows, :]) + 1e-8)

    @pl.when(c == 1)
    def _():
        each(0, ROWS // 128, invert)

    each(READY // PAIR, STEPS, sum_and_send)

    @pl.when(c == 0)
    def _():
        each(0, ROWS // 128, invert)


    def late(t, _):
        @pl.when(t == SERVE)
        def _():
            landed(server_error.at[pl.ds(0, NZ - 1)], server_recv)

        for lag, task in (
            (0, sum_plane),
            (SPREAD, spread),
            (SERVE, serve),
            (SCATTER, scatter),
            (HAND, hand_over),
            (TAKE, take_over),
        ):

            @pl.when(jnp.logical_and(t >= lag, t < lag + STEPS))
            def _():
                task(t - lag)

        return 0

    lax.fori_loop(0, STEPS + TAKE, late, 0)
    server_residue[...] = residue[z]

    landed(from_core, out_sem)
    landed(from_plane.at[:, pl.ds(0, PLANE - 1)], out_sem)
    landed(plane_sum.at[:, pl.ds(0, NZ - 1)], out_sem)
    landed(server_error.at[pl.ds(0, NZ - 1)], out_sem)
    landed(from_plane.at[:, pl.ds(0, PLANE - 1)], out_sem)
    landed(gathered.at[0, pl.ds(0, DIRECT)], out_sem)
    if DIRECT < STEPS:
        landed(gathered.at[0, pl.ds(0, STEPS - DIRECT)], out_sem)


def store(update, worker_error, server_residue, *refs):
    outs, sem = refs[:3], refs[3]
    copies = []
    for i, (src, dst) in enumerate(zip((update, worker_error, server_residue), outs)):
        parts = PARTS if src.shape[0] == ROWS else 1
        rows = src.shape[0] // parts
        for j in range(parts):
            piece = pl.ds(j * rows, rows)
            copies.append(pltpu.make_async_copy(src.at[piece], dst.at[piece], sem.at[i, j]))
    for copy in copies:
        copy.start()
    for copy in copies:
        copy.wait()


def local(grad, momentum, error, variance, server_error):
    f32, bf16, dma = jnp.float32, jnp.bfloat16, pltpu.SemaphoreType.DMA
    whole = (ROWS, 128)
    held = pl.pallas_call(
        kernel,
        name="exchange",
        out_shape=(
            pltpu.VMEM(whole, f32),
            pltpu.VMEM(whole, f32),
            pltpu.VMEM((SPAN, 128), f32),
        ),
        in_specs=[pl.BlockSpec(memory_space=pltpu.HBM)] * 5,
        out_specs=[pl.BlockSpec(memory_space=pltpu.VMEM)] * 3,
        scratch_shapes=[
            pltpu.VMEM((1, ROWS * 128), bf16),
            pltpu.VMEM(whole, f32),
            pltpu.VMEM(whole, f32),
            pltpu.VMEM(whole, f32),
            pltpu.VMEM((NZ, SPAN, 128), f32),
            pltpu.VMEM((NZ, SPAN, 128), f32),
            pltpu.VMEM((2, NZ, PLANE, SPAN, 128), bf16),
            pltpu.VMEM((NZ, PLANE, SPAN, 128), bf16),
            pltpu.VMEM((STEPS, PLANE, PAIR, SPAN, 128), bf16),
            pltpu.VMEM((STEPS, PLANE, PAIR, SPAN, 128), bf16),
            pltpu.VMEM((STEPS, NZ, PAIR, SPAN, 128), bf16),
            pltpu.VMEM((2, STEPS, PLANE, PAIR, SPAN, 128), bf16),
            dma((2, NZ)),
            dma((2,)),
            dma,
            dma, dma((NZ // 2,)),
            dma((STEPS,)),
            dma((STEPS,)),
            pltpu.SemaphoreType.REGULAR,
        ],
        compiler_params=pltpu.CompilerParams(
            collective_id=0, has_side_effects=True, vmem_limit_bytes=32 << 20
        ),
    )(
        *(
            pltpu.with_memory_space_constraint(operand, pltpu.HBM)
            for operand in (
                grad,
                momentum.reshape(whole),
                error.reshape(whole),
                variance.reshape(whole),
                server_error.reshape(SPAN, 128),
            )
        )
    )
    update, worker_error, server_residue = pl.pallas_call(
        store,
        name="store",
        out_shape=tuple(jax.ShapeDtypeStruct(v.shape, v.dtype) for v in held),
        in_specs=[pl.BlockSpec(memory_space=pltpu.VMEM)] * 3,
        out_specs=[pl.BlockSpec(memory_space=pl.ANY)] * 3,
        scratch_shapes=[dma((3, PARTS))],
        compiler_params=pltpu.CompilerParams(vmem_limit_bytes=1 << 20),
    )(*(pltpu.with_memory_space_constraint(v, pltpu.VMEM) for v in held))
    return (
        update.reshape(ROWS * 128),
        worker_error.reshape(1, ROWS * 128),
        server_residue.reshape(SPAN * 128),
    )


def solution(mesh):
    placed = (
        P(("dp", "outer"), None),
        P(("dp", "outer"), None),
        P(("dp", "outer"), None),
        P(),
        P(("dp", "outer")),
    )
    return jax.shard_map(
        local,
        mesh=mesh,
        in_specs=placed,
        out_specs=(P(), P(("dp", "outer"), None), P(("dp", "outer"))),
        check_vma=False,
    )
```

```python
import jax
import jax.numpy as jnp
from jax import lax
from jax.experimental import pallas as pl
from jax.experimental.pallas import tpu as pltpu
from jax.sharding import PartitionSpec as P

MESH = pl.DeviceIdType.MESH
NX, NY, NZ = 4, 4, 8
PLANE = NX * NY
SPAN = 16
CHUNK = 2 * PLANE * SPAN
ROWS = NZ * CHUNK
GREET, MEET = 1, 2
BEFORE, READY = 6, 2
PAIR = 1
STEPS = NZ // PAIR
DIRECT = 7
SPREAD, SERVE, SCATTER, HAND, TAKE = 0, 7, 7, 14, 16
PARTS = 1

AWAY = sorted(
    ((dx, dy) for dx in range(NX) for dy in range(NY) if dx or dy),
    key=lambda d: -min(d[0], NX - d[0]) - min(d[1], NY - d[1]),
)
ABOVE = sorted(range(1, NZ), key=lambda d: -min(d, NZ - d))


def compress(values):
    power = jnp.mean(values * values, axis=-1, keepdims=True) + 1e-6
    inverse = lax.rsqrt(power)
    return power * inverse * jnp.tanh(values * inverse)


def kernel(
    grad_hbm, momentum_hbm, error_hbm, variance_hbm, server_error_hbm,
    update, worker_error, server_residue,
    grad, momentum, error, scale, server_error, residue,
    sent, from_core, chip_sum, from_plane, plane_sum, gathered,
    in_sem, small_sem, server_recv,
    out_sem, core_recv, plane_recv, z_recv, word,
):
    dp = lax.axis_index("dp")
    x = lax.axis_index("outer")
    c = lax.rem(dp, 2)
    y = lax.rem(lax.div(dp, 2), NY)
    z = lax.div(dp, 2 * NY)

    me = y * NX + x

    def at(px, py, pz, pc):
        return ((pz * NY + py) * 2 + pc, px)

    sibling = at(x, y, z, 1 - c)
    plane = [(lax.rem(x + dx, NX), lax.rem(y + dy, NY)) for dx, dy in AWAY]
    column = [lax.rem(z + d, NZ) for d in ABOVE]

    gather_recv, last_recv = in_sem.at[0], in_sem.at[1]

    def remote(src, dst, send, recv, device):
        return pltpu.make_async_remote_copy(
            src, dst, send, recv, device_id=device, device_id_type=MESH
        )

    def landed(like, sem):
        pltpu.make_async_copy(like, like, sem).wait()

    def each(first, end, body):
        def step(k, _):
            body(k)
            return 0

        lax.fori_loop(first, end, step, 0)

    def load_grad(k):
        flat = pl.ds(pl.multiple_of(k * (CHUNK * 128), CHUNK * 128), CHUNK * 128)
        return pltpu.make_async_copy(grad_hbm.at[:, flat], grad.at[:, flat], in_sem.at[0, k])

    def start_loads(k):
        load_grad(k).start()
        rows = pl.ds(pl.multiple_of(k * CHUNK, CHUNK), CHUNK)
        for src, dst in ((momentum_hbm, momentum), (error_hbm, error)):
            pltpu.make_async_copy(src.at[rows], dst.at[rows], in_sem.at[1, k]).start()

    barrier = pltpu.get_barrier_semaphore()
    others = [(x, y, column[0]), *((px, py, z) for px, py in plane), *((x, y, pz) for pz in column[1:])]

    def signal(semaphore, device):
        pl.semaphore_signal(semaphore, inc=1, device_id=device, device_id_type=MESH)

    for other in others:
        signal(barrier, at(*other, 0))

    @pl.when(c == 0)
    def _():
        signal(barrier, sibling)

    start_loads(0)
    load_server = pltpu.make_async_copy(server_error_hbm, server_error.at[z], small_sem.at[0])
    load_server.start()
    each(1, NZ, start_loads)
    load_variance = pltpu.make_async_copy(variance_hbm, scale, small_sem.at[1])
    load_variance.start()

    def compress_chunk(k):
        load_grad(k).wait()
        landed(momentum.at[pl.ds(0, 2 * CHUNK)], in_sem.at[1, k])
        for py in range(NY):
            first = pl.multiple_of(k * CHUNK + py * 128, 128)
            flat = pl.ds(pl.multiple_of(first * 128, 128 * 128), 128 * 128)
            rows = pl.ds(first, 128)
            slope = grad[:, flat].astype(jnp.float32).reshape(128, 128)
            compensated = 0.9 * momentum[rows, :] + 0.1 * slope + error[rows, :]
            rounded = compress(compensated).astype(jnp.bfloat16)
            worker_error[rows, :] = compensated - rounded.astype(jnp.float32)
            for pc in range(2):
                for px in range(NX):
                    first = (pc * NX + px) * SPAN
                    sent[pc, k, py * NX + px] = rounded[first : first + SPAN]

    def send_core(i):
        both = pl.ds(2 * i, 2)
        remote(sent.at[1 - c, both], from_core.at[both], out_sem, core_recv.at[i], sibling).start()

    def sum_chip(k):
        @pl.when(lax.rem(k, 2) == 0)
        def _():
            landed(from_core.at[pl.ds(0, 2)], core_recv.at[lax.div(k, 2)])

        total = sent[c, k].astype(jnp.float32) + from_core[k].astype(jnp.float32)
        chip_sum[lax.div(k, PAIR), :, lax.rem(k, PAIR)] = total.astype(jnp.bfloat16)

    def together(i):
        return pl.ds(i * PAIR, PAIR)

    def members(i):
        return [i * PAIR + j for j in range(PAIR)]

    def send_plane(i):
        for px, py in plane:
            src, dst = chip_sum.at[i, py * NX + px], from_plane.at[i, me]
            remote(src, dst, out_sem, plane_recv.at[i], at(px, py, z, c)).start()
        from_plane[i, me] = chip_sum[i, me]

    def to_plane(i, pz):
        block = plane_sum.at[i, z]
        remote(block, block, out_sem, z_recv.at[i], at(x, y, pz, c)).start()

    def sum_plane(i):
        landed(from_plane.at[i, pl.ds(0, PLANE - 1)], plane_recv.at[i])
        total = jnp.sum(from_plane[i].astype(jnp.float32), axis=0)
        plane_sum[i, z] = total.astype(jnp.bfloat16)

        @pl.when(z != 0)
        def _():
            to_plane(i, 0)

    def spread(i):
        for pz in column:

            @pl.when(pz != 0)
            def _():
                to_plane(i, pz)

    def to_chip(i, px, py):
        block = gathered.at[c, i, me]
        remote(block, block, out_sem, gather_recv.at[i], at(px, py, z, c)).start()

    def serve(i):
        landed(plane_sum.at[i, pl.ds(0, NZ - 1)], z_recv.at[i])
        total = jnp.sum(plane_sum[i].astype(jnp.float32), axis=0)
        shifted = total * (1.0 / (2 * PLANE * NZ)) + server_error[together(i)]
        answer = compress(shifted).astype(jnp.bfloat16)
        gathered[c, i, me] = answer
        residue[together(i)] = shifted - answer.astype(jnp.float32)

        @pl.when(me != 0)
        def _():
            to_chip(i, 0, 0)

    def scatter(i):
        for px, py in plane:

            @pl.when(py * NX + px != 0)
            def _():
                to_chip(i, px, py)

        @pl.when(i >= DIRECT)
        def _():
            block = gathered.at[c, i, me]
            for px, py in plane:
                other = at(px, py, z, 1 - c)
                remote(block, block, out_sem, last_recv.at[i], other).start()
            remote(block, block, out_sem, last_recv.at[i], sibling).start()

    def finish(i, j, pc):
        for py in range(NY):
            first = pl.multiple_of((i * PAIR + j) * CHUNK + py * 128 + pc * 64, 64)
            rows = pl.ds(first, 64)
            values = gathered[pc, i, py * NX : (py + 1) * NX, j].astype(jnp.float32)
            update[rows, :] = values.reshape(64, 128) * scale[rows, :]

    def hand_over(i):
        landed(from_plane.at[i, pl.ds(0, PLANE - 1)], gather_recv.at[i])

        @pl.when(i < DIRECT)
        def _():
            block = gathered.at[c, i]
            remote(block, block, out_sem, last_recv.at[i], sibling).start()

        for j in range(PAIR):
            finish(i, j, c)

    def take_over(i):
        landed(gathered.at[1 - c, i], last_recv.at[i])
        for j in range(PAIR):
            finish(i, j, 1 - c)

    def compress_and_send(k):
        compress_chunk(k)

        @pl.when(lax.rem(k, 2) == 1)
        def _():
            send_core(lax.div(k, 2))

    def sum_and_send(i):
        for k in members(i):
            sum_chip(k)
        send_plane(i)

    each(0, GREET, compress_chunk)

    @pl.when(c == 1)
    def _():
        pl.semaphore_wait(barrier, 1)
        signal(word, sibling)

    each(GREET, MEET, compress_chunk)

    @pl.when(c == 0)
    def _():
        pl.semaphore_wait(word, 1)

    each(0, MEET // 2, send_core)
    each(MEET, BEFORE, compress_and_send)
    each(0, READY, sum_chip)

    @pl.when(c == 0)
    def _():
        pl.semaphore_wait(barrier, 2 * len(others))
        signal(word, sibling)

    @pl.when(c == 1)
    def _():
        pl.semaphore_wait(word, 1)

    each(0, READY // PAIR, send_plane)
    load_server.wait()
    for pz in column:
        block = server_error.at[z]
        remote(block, block, out_sem, server_recv, at(x, y, pz, c)).start()
    each(BEFORE, NZ, compress_and_send)
    load_variance.wait()

    def invert(i):
        rows = pl.ds(pl.multiple_of(i * 128, 128), 128)
        scale[rows, :] = 1.0 / (jnp.sqrt(scale[rows, :]) + 1e-8)

    @pl.when(c == 1)
    def _():
        each(0, ROWS // 128, invert)

    each(READY // PAIR, STEPS, sum_and_send)

    @pl.when(c == 0)
    def _():
        each(0, ROWS // 128, invert)


    def late(t, _):
        @pl.when(t == SERVE)
        def _():
            landed(server_error.at[pl.ds(0, NZ - 1)], server_recv)

        for lag, task in (
            (0, sum_plane),
            (SPREAD, spread),
            (SERVE, serve),
            (SCATTER, scatter),
            (HAND, hand_over),
            (TAKE, take_over),
        ):

            @pl.when(jnp.logical_and(t >= lag, t < lag + STEPS))
            def _():
                task(t - lag)

        return 0

    lax.fori_loop(0, STEPS + TAKE, late, 0)
    server_residue[...] = residue[z]

    landed(from_core, out_sem)
    landed(from_plane.at[:, pl.ds(0, PLANE - 1)], out_sem)
    landed(plane_sum.at[:, pl.ds(0, NZ - 1)], out_sem)
    landed(server_error.at[pl.ds(0, NZ - 1)], out_sem)
    landed(from_plane.at[:, pl.ds(0, PLANE - 1)], out_sem)
    landed(gathered.at[0, pl.ds(0, DIRECT)], out_sem)
    if DIRECT < STEPS:
        landed(gathered.at[0, pl.ds(0, STEPS - DIRECT)], out_sem)


def store(update, worker_error, server_residue, *refs):
    outs, sem = refs[:3], refs[3]
    copies = []
    for i, (src, dst) in enumerate(zip((update, worker_error, server_residue), outs)):
        parts = PARTS if src.shape[0] == ROWS else 1
        rows = src.shape[0] // parts
        for j in range(parts):
            piece = pl.ds(j * rows, rows)
            copies.append(pltpu.make_async_copy(src.at[piece], dst.at[piece], sem.at[i, j]))
    for copy in copies:
        copy.start()
    for copy in copies:
        copy.wait()


def local(grad, momentum, error, variance, server_error):
    f32, bf16, dma = jnp.float32, jnp.bfloat16, pltpu.SemaphoreType.DMA
    whole = (ROWS, 128)
    held = pl.pallas_call(
        kernel,
        name="exchange",
        out_shape=(
            pltpu.VMEM(whole, f32),
            pltpu.VMEM(whole, f32),
            pltpu.VMEM((SPAN, 128), f32),
        ),
        in_specs=[pl.BlockSpec(memory_space=pltpu.HBM)] * 5,
        out_specs=[pl.BlockSpec(memory_space=pltpu.VMEM)] * 3,
        scratch_shapes=[
            pltpu.VMEM((1, ROWS * 128), bf16),
            pltpu.VMEM(whole, f32),
            pltpu.VMEM(whole, f32),
            pltpu.VMEM(whole, f32),
            pltpu.VMEM((NZ, SPAN, 128), f32),
            pltpu.VMEM((NZ, SPAN, 128), f32),
            pltpu.VMEM((2, NZ, PLANE, SPAN, 128), bf16),
            pltpu.VMEM((NZ, PLANE, SPAN, 128), bf16),
            pltpu.VMEM((STEPS, PLANE, PAIR, SPAN, 128), bf16),
            pltpu.VMEM((STEPS, PLANE, PAIR, SPAN, 128), bf16),
            pltpu.VMEM((STEPS, NZ, PAIR, SPAN, 128), bf16),
            pltpu.VMEM((2, STEPS, PLANE, PAIR, SPAN, 128), bf16),
            dma((2, NZ)),
            dma((2,)),
            dma,
            dma, dma((NZ // 2,)),
            dma((STEPS,)),
            dma((STEPS,)),
            pltpu.SemaphoreType.REGULAR,
        ],
        compiler_params=pltpu.CompilerParams(
            collective_id=0, has_side_effects=True, vmem_limit_bytes=32 << 20
        ),
    )(
        *(
            pltpu.with_memory_space_constraint(operand, pltpu.HBM)
            for operand in (
                grad,
                momentum.reshape(whole),
                error.reshape(whole),
                variance.reshape(whole),
                server_error.reshape(SPAN, 128),
            )
        )
    )
    update, worker_error, server_residue = pl.pallas_call(
        store,
        name="store",
        out_shape=tuple(jax.ShapeDtypeStruct(v.shape, v.dtype) for v in held),
        in_specs=[pl.BlockSpec(memory_space=pltpu.VMEM)] * 3,
        out_specs=[pl.BlockSpec(memory_space=pl.ANY)] * 3,
        scratch_shapes=[dma((3, PARTS))],
        compiler_params=pltpu.CompilerParams(vmem_limit_bytes=1 << 20),
    )(*(pltpu.with_memory_space_constraint(v, pltpu.VMEM) for v in held))
    return (
        update.reshape(ROWS * 128),
        worker_error.reshape(1, ROWS * 128),
        server_residue.reshape(SPAN * 128),
    )


def solution(mesh):
    placed = (
        P(("dp", "outer"), None),
        P(("dp", "outer"), None),
        P(("dp", "outer"), None),
        P(),
        P(("dp", "outer")),
    )
    return jax.shard_map(
        local,
        mesh=mesh,
        in_specs=placed,
        out_specs=(P(), P(("dp", "outer"), None), P(("dp", "outer"))),
        check_vma=False,
    )
```
